128 devices in a mesh: gx: 16 (over z, x), gy: 8 (over y, core).
Axes of the slice: x: 4, y: 4, z: 4, core: 2. Of those that a mesh axis runs over, the one named last changes fastest.
Arguments:
- initial_head: float32 [10, 512, 1024], P(None, 'gx', 'gy'), may hold values from -6 to 6
- conductivity: float32 [10, 512, 1024], P(None, 'gx', 'gy'), may hold values from 0.3 to 3
- source_rate: float32 [10, 512, 1024], P(None, 'gx', 'gy'), may hold values from -6 to 6
- storage_term: float32 [10, 512, 1024], P(None, 'gx', 'gy'), may hold values from 0.05 to 0.5
- bed_conduct: float32 [512, 1024], P('gx', 'gy'), may hold values from 0.001 to 0.01
- row_cells: int32 [128, 256, 128], P(('gx', 'gy')), may hold values from 0 to 4096, as said below
- row_reach: int32 [128, 256], P(('gx', 'gy')), may hold values from 0 to 255
- river_section: float32 [128, 256], P(('gx', 'gy')), may hold values from -6 to 6
- bed_depth: float32 [128, 256], P(('gx', 'gy')), may hold values from 0.5 to 2
- route_inverse: float32 [128, 256, 256], P(('gx', 'gy')), as said below
- retention: float32 [128], P(('gx', 'gy')), may hold values from 0.9 to 1
- chain_heads: int32 [128], P(('gx', 'gy')), may hold values 0 or 1
Outputs:
- head_field: float32 [10, 512, 1024], P(None, 'gx', 'gy')
- reach_flow: float32 [128, 256], P(('gx', 'gy'))
The draws below stay inside these ranges and needn't reach their ends.
Inputs may be any that keep to these rules, and one draw needn't show every extreme that they name: `row_cells`: each row lists 1 to 128 cells of the sender's tile followed by the empty index 4096; row 0 of every sender is full. `route_inverse`: each block's matrix is lower triangular with a unit diagonal.
All inputs are finite; a program needn't handle non-finite values. No bound on the sum of `chain_heads` on one device may be relied on, other than what follows from the above.
Results may differ from the reference program's by a relative error of at most 0.00018.
Values sent between devices are 32-bit elements; how exact they have to be, the bound alone decides.
No kernel may reach another device: no remote copies, remote signals or barrier semaphores. Data moves between devices by JAX's collectives and lax.ppermute only.
A program may use at most 64 MiB of HBM per device.

```python
import math
import jax
import jax.numpy as jnp
from jax import lax

LAYERS = 10
CX = 32
CY = 128
SWEEPS = 8
PAD = 128
CAP = 2
R_DEV = 256
NX = 512
NY = 1024
N_GX = 16
N_GY = 8
DEVICES = 128


def draw_row_cells(key, part):
    key = jax.random.fold_in(key, 11)
    key_length, key_cells = jax.random.split(key)
    lengths = jax.random.randint(key_length, (DEVICES, DEVICES * CAP, 1), 1, PAD + 1)
    row_index = jnp.arange(DEVICES * CAP)[None, :, None]
    lengths = jnp.where(row_index == 0, PAD, lengths)
    cells = jax.random.randint(key_cells, (DEVICES, DEVICES * CAP, PAD), 0, CX * CY)
    position = jnp.arange(PAD)[None, None, :]
    return jnp.where(position < lengths, cells, CX * CY).astype(jnp.int32)


def draw_route_inverse(key, part):
    key = jax.random.fold_in(key, 23)
    lowest = 0.2
    values = jax.random.uniform(key, (DEVICES, R_DEV, R_DEV), jnp.float32, lowest, 1.0)
    row_index = jnp.arange(R_DEV)[:, None]
    col_index = jnp.arange(R_DEV)[None, :]
    unit = jnp.where(row_index == col_index, 1.0, 0.0).astype(jnp.float32)
    return jnp.where(row_index > col_index, values, unit)[None].reshape(DEVICES, R_DEV, R_DEV).astype(jnp.float32)


def touch_ends(values, own_key, low, high):
    longest = values.shape.index(max(values.shape))
    spots = []
    for shift in (0, 1):
        where = [jax.random.randint(jax.random.fold_in(own_key, axis), (), 0, length) for axis, length in enumerate(values.shape)]
        where[longest] = (where[longest] + shift) % values.shape[longest]
        spots.append(tuple(where))
    return values.at[spots[0]].set(low).at[spots[1]].set(high)


def levels(rng, extent, cuts, low, largest):
    factor_of = 1.0
    for axis_at, blocks in cuts:
        heights = jax.random.uniform(jax.random.fold_in(jax.random.fold_in(rng, 6), axis_at), (blocks,), jnp.float32, low / len(cuts), largest / len(cuts))
        factor_of = factor_of * jnp.repeat(jnp.exp(heights), extent[axis_at] // blocks).reshape((-1,) + (1,) * (len(extent) - 1 - axis_at))
    return factor_of


def centred(stream_key, dims, scale, most, shards=(), held_as=jnp.bfloat16):
    level = levels(stream_key, dims, shards, -0.22, 0.18) if shards else 1.0
    array = jax.random.normal(stream_key, dims, jnp.float32) * scale * level
    return jnp.minimum(jnp.maximum(array, -most), most).astype(held_as)


def setup_inputs(seed: int = 0) -> dict:
    key_list = jax.random.split(jax.random.key(seed), 13)
    return {
        "initial_head": centred(key_list[0], (LAYERS, NX, NY), 1.0, 6.0, ((1, 16), (2, 8)), jnp.float32),
        "conductivity": jnp.clip(jnp.exp(math.log(3.0) - 2.3025851 * jax.random.uniform(key_list[1], (LAYERS, NX, NY), jnp.float32) ** levels(key_list[1], (LAYERS, NX, NY), ((1, 16), (2, 8)), -0.2, 0.2)), 0.3, 3.0),
        "source_rate": centred(key_list[2], (LAYERS, NX, NY), 1.0, 6.0, ((1, 16), (2, 8)), jnp.float32),
        "storage_term": jnp.clip(jnp.exp(math.log(0.5) - 2.3025851 * jax.random.uniform(key_list[3], (LAYERS, NX, NY), jnp.float32) ** levels(key_list[3], (LAYERS, NX, NY), ((1, 16), (2, 8)), -0.2, 0.2)), 0.05, 0.5),
        "bed_conduct": jnp.clip(jnp.exp(math.log(0.01) - 2.30258502 * jax.random.uniform(key_list[4], (NX, NY), jnp.float32) ** levels(key_list[4], (NX, NY), ((0, 16), (1, 8)), -0.2, 0.2)), 0.001, 0.01),
        "row_cells": draw_row_cells(jax.random.fold_in(key_list[12], 71), 0),
        "row_reach": touch_ends(jax.random.randint(key_list[6], (DEVICES, DEVICES * CAP), 0, R_DEV), jax.random.fold_in(key_list[6], 1), 0, R_DEV - 1).astype(jnp.int32),
        "river_section": centred(key_list[7], (DEVICES, R_DEV), 1.0, 6.0, ((0, 128),), jnp.float32),
        "bed_depth": jnp.clip(0.5 + 1.5 * jax.random.uniform(key_list[8], (DEVICES, R_DEV), jnp.float32) ** levels(key_list[8], (DEVICES, R_DEV), ((0, 128),), -0.2, 0.2), 0.5, 2.0),
        "route_inverse": draw_route_inverse(jax.random.fold_in(key_list[12], 71), 0),
        "retention": jnp.clip(jnp.exp(math.log(1.0) - 0.105360542 * jax.random.uniform(key_list[10], (DEVICES,), jnp.float32) ** levels(key_list[10], (DEVICES,), ((0, 128),), -0.2, 0.2)), 0.9, 1.0),
        "chain_heads": touch_ends((jax.random.randint(key_list[11], (DEVICES,), 0, 16) < 1).astype(jnp.int32), jax.random.fold_in(key_list[11], 1), 0, 1),
    }


def relax(head_pad, cond_pad, mask_pad, source, storage):
    height = head_pad.shape[1] - 2
    breadth = head_pad.shape[2] - 2
    cond_mid = cond_pad[:, 1:-1, 1:-1]
    head_mid = head_pad[:, 1:-1, 1:-1]
    mask_mid = mask_pad[:, 1:-1, 1:-1]
    numerator = source
    denominator = storage
    for offset_x, offset_y in ((0, 1), (2, 1), (1, 0), (1, 2)):
        cond_near = cond_pad[:, offset_x:offset_x + height, offset_y:offset_y + breadth]
        head_near = head_pad[:, offset_x:offset_x + height, offset_y:offset_y + breadth]
        mask_near = mask_pad[:, offset_x:offset_x + height, offset_y:offset_y + breadth]
        face = 0.5 * (cond_mid + cond_near) * mask_near
        numerator = numerator + face * head_near
        denominator = denominator + face
    vertical = 0.5 * (cond_mid[1:] + cond_mid[:-1])
    nothing = jnp.zeros_like(cond_mid[:1])
    numerator = numerator + jnp.concatenate([nothing, vertical * head_mid[:-1]], 0) + jnp.concatenate([vertical * head_mid[1:], nothing], 0)
    denominator = denominator + jnp.concatenate([nothing, vertical], 0) + jnp.concatenate([vertical, nothing], 0)
    return numerator / (denominator + (1.0 - mask_mid)) * mask_mid


def pad_plane(field):
    return jnp.pad(field, ((0, 0), (1, 1), (1, 1)))


def reference(initial_head, conductivity, source_rate, storage_term, bed_conduct, row_cells, row_reach, river_section, bed_depth, route_inverse, retention, chain_heads):
    mask_pad = pad_plane(jnp.ones((1, NX, NY), jnp.float32))
    cond_pad = pad_plane(conductivity)
    head_now = initial_head
    for sweep_index in range(SWEEPS):
        head_now = relax(pad_plane(head_now), cond_pad, mask_pad, source_rate, storage_term)
    head_field = head_now

    def tiled(plane):
        tiles = plane.reshape(N_GX, CX, N_GY, CY).transpose(0, 2, 1, 3).reshape(DEVICES, CX * CY)
        return jnp.concatenate([tiles, jnp.zeros((DEVICES, 1), jnp.float32)], 1)

    flat_cells = row_cells.reshape(DEVICES, DEVICES * CAP * PAD)
    head_rows = jnp.take_along_axis(tiled(head_field[0]), flat_cells, 1)
    bed_rows = jnp.take_along_axis(tiled(bed_conduct), flat_cells, 1)
    head_rows = head_rows.reshape(DEVICES, DEVICES, CAP, PAD).transpose(1, 0, 2, 3).reshape(DEVICES, DEVICES * CAP, PAD)
    bed_rows = bed_rows.reshape(DEVICES, DEVICES, CAP, PAD).transpose(1, 0, 2, 3).reshape(DEVICES, DEVICES * CAP, PAD)
    section_row = jnp.take_along_axis(river_section, row_reach, 1)
    bottom_row = section_row - jnp.take_along_axis(bed_depth, row_reach, 1)
    leak = bed_rows * (jnp.maximum(head_rows, bottom_row[..., None]) - section_row[..., None])
    row_leak = jnp.sum(leak, -1)

    def per_block(values, reaches):
        return jax.ops.segment_sum(values, reaches, num_segments=R_DEV)

    reach_leak = jax.vmap(per_block)(row_leak, row_reach)
    local_flow = jnp.einsum("dij,dj->di", route_inverse, reach_leak, precision=lax.Precision.HIGHEST)
    carry = retention * (1.0 - chain_heads.astype(jnp.float32))

    def chain_step(outlet_prev, pieces):
        carry_here, last_here = pieces
        inflow_here = carry_here * outlet_prev
        return last_here + inflow_here, inflow_here

    start = jnp.zeros((), jnp.float32)
    final_outlet, inflow = lax.scan(chain_step, start, (carry, local_flow[:, -1]))
    reach_flow = local_flow + inflow[:, None]
    return head_field, reach_flow
```

```python
import jax
import jax.numpy as jnp
from jax import lax
from jax.experimental import pallas as pl
from jax.experimental.pallas import tpu as pltpu
from jax.sharding import PartitionSpec as P

SWEEPS = 8
HALO = 8
LANES = 128
GROUPS = LANES // HALO
AXES = ("gx", "gy")
VMEM = pl.BlockSpec(memory_space=pltpu.VMEM)
SMEM = pl.BlockSpec(memory_space=pltpu.SMEM)


def call(body, out, count, scratch=(), smem=(), cost=None):
    return pl.pallas_call(
        body,
        out_shape=out,
        in_specs=[SMEM if i in smem else VMEM for i in range(count)],
        out_specs=jax.tree.map(lambda _: VMEM, out),
        scratch_shapes=list(scratch),
        compiler_params=pltpu.CompilerParams(vmem_limit_bytes=40 * 1024 * 1024),
        cost_estimate=cost,
    )


def f32(*shape):
    return jax.ShapeDtypeStruct(shape, jnp.float32)


def pack_x(head, cond, source, storage, last_out, first_out):
    rows = head.shape[1]
    for k, ref in enumerate((head, cond, source, storage)):
        last_out[k] = ref[:, rows - HALO :, :]
        first_out[k] = ref[:, :HALO, :]


def pack_y(head, cond, source, storage, low, high, last_out, first_out):
    layers, rows, width = head.shape
    lane = lax.broadcasted_iota(jnp.int32, (rows + 2 * HALO, LANES), 1)
    first_sum = [None] * last_out.shape[0]
    last_sum = [None] * last_out.shape[0]
    for k, ref in enumerate((head, cond, source, storage)):
        for l in range(layers):
            plane, group = divmod(k * layers + l, GROUPS)
            whole = jnp.concatenate([ref[l], high[k, l], low[k, l]], 0)
            mine = (lane >= group * HALO) & (lane < (group + 1) * HALO)
            first = pltpu.roll(whole, group * HALO, 1) if group else whole
            turn = (group + 1) * HALO % LANES
            last = pltpu.roll(whole, turn, 1) if turn else whole
            if first_sum[plane] is None:
                first_sum[plane], last_sum[plane] = first, last
            else:
                first_sum[plane] = jnp.where(mine, first, first_sum[plane])
                last_sum[plane] = jnp.where(mine, last, last_sum[plane])
    for plane in range(last_out.shape[0]):
        first_out[plane] = first_sum[plane]
        last_out[plane] = last_sum[plane]


def row_info(reach, section, depth, route, retention, heads, info_out, routed_out):
    rows = reach.shape[1]
    reaches = section.shape[1]
    carry = retention[0] * (1.0 - heads[0].astype(jnp.float32))
    sec = section[...]
    bottom = sec - depth[...]
    weight = route[reaches - 1 : reaches, :]
    stacked = jnp.concatenate(
        [sec, bottom, weight, jnp.zeros((LANES - 3, reaches), jnp.float32)], 0
    )
    line = lax.broadcasted_iota(jnp.int32, (reaches, rows), 0)
    one_hot = (line == reach[...]).astype(jnp.float32)
    picked = jnp.dot(
        stacked[:8], one_hot, precision=lax.Precision.HIGHEST, preferred_element_type=jnp.float32
    )
    kind = lax.broadcasted_iota(jnp.int32, (8, rows), 0)
    picked = jnp.where(kind == 3, carry, picked)
    picked = jnp.concatenate([picked, jnp.zeros((LANES - 8, rows), jnp.float32)], 0)
    for part in range(rows // LANES):
        info_out[part * LANES : (part + 1) * LANES, :] = jnp.transpose(
            picked[:, part * LANES : (part + 1) * LANES]
        )
    routed_out[...] = lax.dot_general(
        one_hot,
        route[...],
        (((0,), (1,)), ((), ())),
        precision=lax.Precision.HIGHEST,
        preferred_element_type=jnp.float32,
    )


def select_cells(cells_ref, table, per_group, finish):
    table_rows = table.shape[0]
    blocks = cells_ref.shape[0] // 8
    for start in range(0, blocks, per_group):
        cells = [cells_ref[(start + b) * 8 : (start + b + 1) * 8, :] for b in range(per_group)]
        column = [c & (LANES - 1) for c in cells]
        line = [c // LANES for c in cells]
        found = [jnp.zeros((8, LANES), jnp.float32) for _ in cells]
        for r in range(table_rows):
            spread = jnp.broadcast_to(table[r : r + 1, :], (8, LANES))
            for b in range(per_group):
                value = jnp.take_along_axis(spread, column[b], axis=1, mode="promise_in_bounds")
                found[b] = jnp.where(line[b] == r, value, found[b])
        for b in range(per_group):
            finish(start + b, found[b])


def pick_beds(cells, bed, out):
    table = bed[...]

    def finish(b, value):
        out[b * 8 : (b + 1) * 8, :] = value

    select_cells(cells, table, 8, finish)


def main(
    head, cond, source, storage, low, high, left, right, cells, beds, info, field_out, send_out,
    now, before, coef, weights,
):
    layers, rows, width = head.shape
    tall = rows + 2 * HALO
    blocks = cells.shape[0] // 8
    peers = cells.shape[0] // 2

    lane1 = lax.broadcasted_iota(jnp.int32, (tall, LANES), 1)

    def extended(k, ref, l):
        plane, group = divmod(k * layers + l, GROUPS)
        whole = jnp.concatenate([ref[l], high[k, l], low[k, l]], 0)
        after = right[plane]
        if group:
            after = pltpu.roll(after, LANES - group * HALO, 1)
        ahead = left[plane]
        turn = (LANES - HALO - group * HALO) % LANES
        if turn:
            ahead = pltpu.roll(ahead, turn, 1)
        side = jnp.where(lane1 < HALO, after, jnp.where(lane1 >= LANES - HALO, ahead, 0.0))
        return jnp.concatenate([whole, side], 1)

    wide = 2 * LANES
    conds = [None, extended(1, cond, 0), None]
    for l in range(layers):
        conds[0], conds[1] = (conds[1], conds[2]) if l else (None, conds[1])
        conds[2] = extended(1, cond, l + 1) if l + 1 < layers else None
        mid = conds[1]
        inside = mid > 0.0

        def face(near):
            return jnp.where(inside & (near > 0.0), 0.5 * (mid + near), 0.0)

        faces = [
            face(pltpu.roll(mid, wide - 1, 1)),
            face(pltpu.roll(mid, 1, 1)),
            face(pltpu.roll(mid, tall - 1, 0)),
            face(pltpu.roll(mid, 1, 0)),
        ]
        faces.append(0.5 * (mid + conds[0]) if l else None)
        faces.append(0.5 * (mid + conds[2]) if l + 1 < layers else None)
        total = extended(3, storage, l)
        for one in faces:
            if one is not None:
                total = total + one
        inverse = jnp.where(inside, 1.0 / jnp.where(inside, total, 1.0), 0.0)
        for k, one in enumerate(faces):
            if one is not None:
                coef[k, l] = one * inverse
        coef[6, l] = extended(2, source, l) * inverse
        now[l] = extended(0, head, l)

    sub = lax.broadcasted_iota(jnp.int32, (peers, LANES), 0)
    lane = lax.broadcasted_iota(jnp.int32, (peers, LANES), 1)
    carry_column = info[pl.ds(0, peers, stride=2), :][:, 3:4]
    carry_row = jnp.sum(jnp.where(sub == lane, carry_column, 0.0), 0, keepdims=True)
    product = jnp.where(lane > sub, carry_row, 1.0)
    step = 1
    while step < LANES:
        product = product * jnp.where(lane >= step, pltpu.roll(product, step, 1), 1.0)
        step *= 2
    product = jnp.where(lane > sub, product, 0.0)
    for c in range(2):
        weights[c] = product * info[pl.ds(c, peers, stride=2), :][:, 2:3]

    def sweep(src, dst):
        for l in range(layers):
            mid = src[l]
            out = coef[6, l] + coef[0, l] * pltpu.roll(mid, wide - 1, 1)
            out = out + coef[1, l] * pltpu.roll(mid, 1, 1)
            out = out + coef[2, l] * pltpu.roll(mid, tall - 1, 0)
            out = out + coef[3, l] * pltpu.roll(mid, 1, 0)
            if l:
                out = out + coef[4, l] * src[l - 1]
            if l + 1 < layers:
                out = out + coef[5, l] * src[l + 1]
            dst[l] = out

    def two_sweeps(_, carry):
        sweep(now, before)
        sweep(before, now)
        return carry

    lax.fori_loop(0, SWEEPS // 2, two_sweeps, 0)
    for l in range(layers):
        field_out[l] = now[l, :rows, :width]

    table = now[0, :rows, :width]
    leaks = [None] * blocks

    def finish(b, value):
        span = pl.ds(b * 8, 8)
        detail = info[span, :]
        leak = beds[span, :] * (jnp.maximum(value, detail[:, 1:2]) - detail[:, 0:1])
        leaks[b] = jnp.sum(leak, 1, keepdims=True)

    select_cells(cells, table, 8, finish)
    row_leak = jnp.concatenate(leaks, 0)
    lane2 = lax.broadcasted_iota(jnp.int32, (2 * peers, LANES), 1)
    send_out[...] = jnp.where(lane2 == 0, row_leak, 0.0)
    flow = jnp.zeros((peers, LANES), jnp.float32)
    for c in range(2):
        flow = flow + weights[c] * send_out[pl.ds(c, peers, stride=2), :][:, 0:1]
    flow = jnp.sum(flow, 0, keepdims=True)
    column = jnp.sum(jnp.where(sub == lane, flow, 0.0), 1, keepdims=True)
    even = send_out[pl.ds(0, peers, stride=2), :]
    send_out[pl.ds(0, peers, stride=2), :] = jnp.where(lane == 1, column, even)


def finish_flow(arrived, routed, out):
    parts = arrived[...]
    flow = jnp.sum(parts[:, 0:1] * routed[...], 0, keepdims=True)
    inflow = jnp.sum(parts[:, 1:2], 0, keepdims=True)
    out[...] = flow + inflow


def shifted(value, axis, by):
    count = lax.axis_size(axis)
    pairs = [(i, i + by) for i in range(count) if 0 <= i + by < count]
    return lax.ppermute(value, axis, pairs)


def per_device(
    initial_head, conductivity, source_rate, storage_term, bed_conduct, row_cells, row_reach,
    river_section, bed_depth, route_inverse, retention, chain_heads,
):
    layers, rows, width = initial_head.shape
    fields = (initial_head, conductivity, source_rate, storage_term)
    edge = f32(4, layers, HALO, width)
    planes = -(-4 * layers // GROUPS)
    side = f32(planes, rows + 2 * HALO, LANES)
    tall = rows + 2 * HALO
    row_total = row_cells.shape[1]
    cells = row_cells[0]

    info, routed = call(
        row_info, (f32(row_total, LANES), f32(row_total, river_section.shape[1])), 6, smem=(4, 5)
    )(row_reach, river_section, bed_depth, route_inverse[0], retention, chain_heads)
    last, first = call(pack_x, (edge, edge), 4)(*fields)
    low = shifted(last, "gx", 1)
    high = shifted(first, "gx", -1)
    info = lax.all_to_all(info, AXES, split_axis=0, concat_axis=0, tiled=True)
    beds = call(pick_beds, f32(row_total, LANES), 2)(cells, bed_conduct)
    last, first = call(pack_y, (side, side), 6)(*fields, low, high)
    left = shifted(last, "gy", 1)
    right = shifted(first, "gy", -1)
    wide = pltpu.VMEM((layers, tall, 2 * LANES), jnp.float32)
    head_field, sent = call(
        main,
        (f32(layers, rows, width), f32(row_total, LANES)),
        11,
        scratch=(
            wide,
            wide,
            pltpu.VMEM((7, layers, tall, 2 * LANES), jnp.float32),
            pltpu.VMEM((2, row_total // 2, LANES), jnp.float32),
        ),
    )(*fields, low, high, left, right, cells, beds, info)
    arrived = lax.all_to_all(sent, AXES, split_axis=0, concat_axis=0, tiled=True)
    reach_flow = call(finish_flow, f32(1, river_section.shape[1]), 2)(arrived, routed)
    return (head_field, reach_flow)


def solution(mesh):
    placed = (
        P(None, "gx", "gy"),
        P(None, "gx", "gy"),
        P(None, "gx", "gy"),
        P(None, "gx", "gy"),
        P("gx", "gy"),
        P(AXES, None, None),
        P(AXES, None),
        P(AXES, None),
        P(AXES, None),
        P(AXES, None, None),
        P(AXES),
        P(AXES),
    )
    return jax.shard_map(
        per_device,
        mesh=mesh,
        in_specs=placed,
        out_specs=(P(None, "gx", "gy"), P(AXES, None)),
        check_vma=False,
    )
```

```python
import jax
import jax.numpy as jnp
from jax import lax
from jax.experimental import pallas as pl
from jax.experimental.pallas import tpu as pltpu
from jax.sharding import PartitionSpec as P

SWEEPS = 8
HALO = 8
LANES = 128
GROUPS = LANES // HALO
AXES = ("gx", "gy")
VMEM = pl.BlockSpec(memory_space=pltpu.VMEM)
ANY = pl.BlockSpec(memory_space=pl.ANY)
TOP, BOTTOM = HALO, 2 * HALO


def call(body, out, count, scratch=(), anywhere=False, mib=8, micros=1):
    return pl.pallas_call(
        body,
        out_shape=out,
        in_specs=[ANY if anywhere else VMEM] * count,
        out_specs=jax.tree.map(lambda _: VMEM, out),
        scratch_shapes=list(scratch),
        compiler_params=pltpu.CompilerParams(vmem_limit_bytes=mib * 1024 * 1024),
        cost_estimate=pl.CostEstimate(
            flops=0, transcendentals=0, bytes_accessed=micros * 3_000_000
        ),
    )


def f32(*shape):
    return jax.ShapeDtypeStruct(shape, jnp.float32)


def front(
    head, cond, source, storage, reach, section, depth, route, retention, heads,
    last_out, first_out, info_out,
    reach_here, section_here, depth_here, weight_here, retention_here, heads_here, sems,
):
    rows = head.shape[1]
    reaches = section.shape[1]
    edges = []
    for k, ref in enumerate((head, cond, source, storage)):
        edges.append((ref.at[:, rows - HALO :, :], last_out.at[k]))
        edges.append((ref.at[:, :HALO, :], first_out.at[k]))
    small = [
        (reach, reach_here),
        (section, section_here),
        (depth, depth_here),
        (route.at[0, reaches - 8 :, :], weight_here),
        (retention, retention_here),
        (heads, heads_here),
    ]
    copies = [pltpu.make_async_copy(a, b, sems.at[i]) for i, (a, b) in enumerate(small + edges)]
    for copy in copies:
        copy.start()
    for copy in copies[: len(small)]:
        copy.wait()
    carry = retention_here[0] * (1.0 - heads_here[0].astype(jnp.float32))
    sec = section_here[...]
    table = jnp.concatenate(
        [sec, sec - depth_here[...], weight_here[7:8, :], jnp.full((5, reaches), carry)], 0
    )
    count = reach.shape[1]
    for part in range(count // LANES):
        spots = jnp.broadcast_to(reach_here[:, part * LANES : (part + 1) * LANES], (8, LANES))
        picked = jnp.zeros((8, LANES), jnp.float32)
        for block in range(reaches // LANES):
            value = jnp.take_along_axis(
                table[:, block * LANES : (block + 1) * LANES],
                spots & (LANES - 1),
                axis=1,
                mode="promise_in_bounds",
            )
            picked = jnp.where(spots // LANES == block, value, picked)
        tall = jnp.concatenate([picked, jnp.zeros((LANES - 8, LANES), jnp.float32)], 0)
        info_out[part * LANES : (part + 1) * LANES, :] = jnp.transpose(tall)
    for copy in copies[len(small) :]:
        copy.wait()


def pack_y(head, cond, source, storage, low, high, last_out, first_out):
    layers, rows, width = head.shape
    lane = lax.broadcasted_iota(jnp.int32, (rows + 2 * HALO, LANES), 1)
    first_sum = [None] * last_out.shape[0]
    last_sum = [None] * last_out.shape[0]
    for k, ref in enumerate((head, cond, source, storage)):
        for l in range(layers):
            plane, group = divmod(k * layers + l, GROUPS)
            whole = jnp.concatenate([low[k, l], ref[l], high[k, l]], 0)
            mine = (lane >= group * HALO) & (lane < (group + 1) * HALO)
            first = pltpu.roll(whole, group * HALO, 1) if group else whole
            turn = (group + 1) * HALO % LANES
            last = pltpu.roll(whole, turn, 1) if turn else whole
            if first_sum[plane] is None:
                first_sum[plane], last_sum[plane] = first, last
            else:
                first_sum[plane] = jnp.where(mine, first, first_sum[plane])
                last_sum[plane] = jnp.where(mine, last, last_sum[plane])
    for plane in range(last_out.shape[0]):
        first_out[plane] = first_sum[plane]
        last_out[plane] = last_sum[plane]


def select_cells(cells_ref, table, finish):
    for b in range(cells_ref.shape[0] // 8):
        cells = cells_ref[b * 8 : (b + 1) * 8, :]
        column, line = cells & (LANES - 1), cells // LANES
        found = jnp.zeros((8, LANES), jnp.float32)
        for r, spread in enumerate(table):
            value = jnp.take_along_axis(spread, column, axis=1, mode="promise_in_bounds")
            found = jnp.where(line == r, value, found)
        finish(b, found)


def spread_rows(table):
    return [jnp.broadcast_to(table[r : r + 1, :], (8, LANES)) for r in range(table.shape[0])]


def pick_beds(cells, bed, out):
    def finish(b, value):
        out[b * 8 : (b + 1) * 8, :] = value

    select_cells(cells, spread_rows(bed[...]), finish)


def extended(fields, halos, k, l):
    low, high, left, right = halos
    layers, rows, width = fields[k].shape
    lane = lax.broadcasted_iota(jnp.int32, (rows + 2 * HALO, LANES), 1)
    plane, group = divmod(k * layers + l, GROUPS)
    whole = jnp.concatenate([low[k, l], fields[k][l], high[k, l]], 0)
    after = right[plane]
    if group:
        after = pltpu.roll(after, LANES - group * HALO, 1)
    ahead = left[plane]
    turn = (LANES - HALO - group * HALO) % LANES
    if turn:
        ahead = pltpu.roll(ahead, turn, 1)
    side = jnp.where(lane < HALO, after, jnp.where(lane >= LANES - HALO, ahead, 0.0))
    return whole, side


def beside(pair):
    lane = lax.broadcasted_iota(jnp.int32, pair[0].shape, 1)
    ahead = [pltpu.roll(one, LANES - 1, 1) for one in pair]
    behind = [pltpu.roll(one, 1, 1) for one in pair]
    east = [jnp.where(lane == LANES - 1, ahead[1 - t], ahead[t]) for t in range(2)]
    west = [jnp.where(lane == 0, behind[1 - t], behind[t]) for t in range(2)]
    return east, west


def set_conduct(fields, halos, conds, l, slot):
    rows = conds.shape[2]
    for t, value in enumerate(extended(fields, halos, 1, l)):
        conds[t, slot, TOP : rows - TOP, :] = value
        conds[t, slot, :TOP, :] = jnp.zeros((TOP, LANES), jnp.float32)
        conds[t, slot, rows - TOP :, :] = jnp.zeros((TOP, LANES), jnp.float32)


def set_coefs(fields, halos, conds, slots, coef, l, at):
    rows = conds.shape[2]
    above, here, below = slots
    mids = [conds[t, here, TOP : rows - TOP, :] for t in range(2)]
    east, west = beside(mids)
    storage = extended(fields, halos, 3, l)
    source = extended(fields, halos, 2, l)
    for t in range(2):
        mid = mids[t]
        inside = mid > 0.0

        def face(near):
            return jnp.where(inside & (near > 0.0), 0.5 * (mid + near), 0.0)

        faces = [
            face(east[t]),
            face(west[t]),
            face(conds[t, here, TOP + 1 : rows - TOP + 1, :]),
            face(conds[t, here, TOP - 1 : rows - TOP - 1, :]),
            None if above is None else 0.5 * (mid + conds[t, above, TOP : rows - TOP, :]),
            None if below is None else 0.5 * (mid + conds[t, below, TOP : rows - TOP, :]),
        ]
        total = storage[t]
        for one in faces:
            if one is not None:
                total = total + one
        inverse = jnp.where(inside, 1.0 / jnp.where(inside, total, 1.0), 0.0)
        for k, one in enumerate(faces):
            if one is not None:
                coef[k, t, at] = one * inverse
        coef[6, t, at] = source[t] * inverse


def sweep(place, coef_of, time, first, last, top, only_main, store):
    for start in range(BOTTOM if only_main else TOP, top - (BOTTOM if only_main else TOP), 8):
        span = slice(start, start + 8)
        mids = {}
        for l in range(max(first - 1, 0), last + 2):
            if place(time, l) is not None:
                ref, at = place(time, l)
                mids[l] = [
                    ref[(*at, t, l, span, slice(None))] for t in range(2)
                ]
        for l in range(first, last + 1):
            ref, at = place(time, l)
            east, west = beside(mids[l])
            coef, c = coef_of(l)
            for t in range(1 if only_main else 2):
                rows = slice(start - TOP, start - TOP + 8)
                out = coef[6, t, c, rows, :] + coef[0, t, c, rows, :] * east[t]
                out = out + coef[1, t, c, rows, :] * west[t]
                out = out + coef[2, t, c, rows, :] * ref[(*at, t, l, slice(start + 1, start + 9), slice(None))]
                out = out + coef[3, t, c, rows, :] * ref[(*at, t, l, slice(start - 1, start + 7), slice(None))]
                if l - 1 in mids:
                    out = out + coef[4, t, c, rows, :] * mids[l - 1][t]
                if l + 1 in mids:
                    out = out + coef[5, t, c, rows, :] * mids[l + 1][t]
                store(l, t, start, out)


def set_heads(fields, halos, heads, l):
    rows = heads.shape[3]
    for t, value in enumerate(extended(fields, halos, 0, l)):
        heads[0, t, l, TOP : rows - TOP, :] = value
        for parity in range(2):
            heads[parity, t, l, :TOP, :] = jnp.zeros((TOP, LANES), jnp.float32)
            heads[parity, t, l, rows - TOP :, :] = jnp.zeros((TOP, LANES), jnp.float32)


def upper(
    head, cond, source, storage, low, high, left, right, cells, beds, info,
    send_out, heads, coef, conds, weights,
):
    fields, halos = (head, cond, source, storage), (low, high, left, right)
    layers, rows, width = head.shape
    peers = cells.shape[0] // 2
    for l in range(SWEEPS + 1):
        set_heads(fields, halos, heads, l)
        set_conduct(fields, halos, conds, l, l)
    for l in range(SWEEPS):
        set_coefs(fields, halos, conds, (l - 1 if l else None, l, l + 1), coef, l, l)

    sub = lax.broadcasted_iota(jnp.int32, (peers, LANES), 0)
    lane = lax.broadcasted_iota(jnp.int32, (peers, LANES), 1)
    carry_column = info[pl.ds(0, peers, stride=2), :][:, 3:4]
    carry_row = jnp.sum(jnp.where(sub == lane, carry_column, 0.0), 0, keepdims=True)
    product = jnp.where(lane > sub, carry_row, 1.0)
    step = 1
    while step < LANES:
        product = product * jnp.where(lane >= step, pltpu.roll(product, step, 1), 1.0)
        step *= 2
    product = jnp.where(lane > sub, product, 0.0)
    for c in range(2):
        weights[c] = product * info[pl.ds(c, peers, stride=2), :][:, 2:3]

    for time in range(SWEEPS):

        def store(l, t, start, value):
            heads[(time + 1) % 2, t, l, start : start + 8, :] = value

        sweep(
            lambda when, l: (heads, (when % 2,)),
            lambda l: (coef, l),
            time, 0, SWEEPS - 1 - time, heads.shape[3], time == SWEEPS - 1, store,
        )

    table = heads[SWEEPS % 2, 0, 0, BOTTOM : BOTTOM + rows, :]
    leaks = []

    def finish(b, value):
        span = pl.ds(b * 8, 8)
        detail = info[span, :]
        leak = beds[span, :] * (jnp.maximum(value, detail[:, 1:2]) - detail[:, 0:1])
        leaks.append(jnp.sum(leak, 1, keepdims=True))

    select_cells(cells, spread_rows(table), finish)
    row_leak = jnp.concatenate(leaks, 0)
    lane2 = lax.broadcasted_iota(jnp.int32, (2 * peers, LANES), 1)
    send_out[...] = jnp.where(lane2 == 0, row_leak, 0.0)
    flow = jnp.zeros((peers, LANES), jnp.float32)
    for c in range(2):
        flow = flow + weights[c] * send_out[pl.ds(c, peers, stride=2), :][:, 0:1]
    flow = jnp.sum(flow, 0, keepdims=True)
    column = jnp.sum(jnp.where(sub == lane, flow, 0.0), 1, keepdims=True)
    even = send_out[pl.ds(0, peers, stride=2), :]
    send_out[pl.ds(0, peers, stride=2), :] = jnp.where(lane == 1, column, even)


def lower(
    head, cond, source, storage, low, high, left, right, heads, reach, route,
    field_out, routed_out, mine, coef, conds,
):
    fields, halos = (head, cond, source, storage), (low, high, left, right)
    layers, rows, width = head.shape
    for l in range(SWEEPS + 1, layers):
        set_heads(fields, halos, mine, l)
    for l in range(1, SWEEPS + 1):
        for t in range(2):
            for parity in range(2):
                mine[parity, t, l, :TOP, :] = jnp.zeros((TOP, LANES), jnp.float32)
                mine[parity, t, l, mine.shape[3] - TOP :, :] = jnp.zeros((TOP, LANES), jnp.float32)
    for l in range(layers):
        set_conduct(fields, halos, conds, l, l)
    for l in range(1, layers):
        set_coefs(
            fields, halos, conds, (l - 1, l, l + 1 if l + 1 < layers else None), coef, l, l
        )

    def place(when, l):
        if l >= layers:
            return None
        return (heads if l <= SWEEPS and when <= SWEEPS - l else mine), (when % 2,)

    for time in range(SWEEPS):
        final = time == SWEEPS - 1

        def store(l, t, start, value):
            if final:
                field_out[l, start - BOTTOM : start - BOTTOM + 8, :] = value
            else:
                mine[(time + 1) % 2, t, l, start : start + 8, :] = value

        sweep(
            place,
            lambda l: (coef, l),
            time, SWEEPS - time, layers - 1, heads.shape[3], final, store,
        )
    field_out[0] = heads[SWEEPS % 2, 0, 0, BOTTOM : BOTTOM + rows, :]
    count, reaches = routed_out.shape
    line = lax.broadcasted_iota(jnp.int32, (reaches, count), 0)
    routed_out[...] = lax.dot_general(
        (line == reach[...]).astype(jnp.float32),
        route[...],
        (((0,), (1,)), ((), ())),
        precision=lax.Precision.HIGHEST,
        preferred_element_type=jnp.float32,
    )


def finish_flow(arrived, routed, out):
    parts = arrived[...]
    flow = jnp.sum(parts[:, 0:1] * routed[...], 0, keepdims=True)
    inflow = jnp.sum(parts[:, 1:2], 0, keepdims=True)
    out[...] = flow + inflow


def shifted(value, axis, by):
    count = lax.axis_size(axis)
    pairs = [(i, i + by) for i in range(count) if 0 <= i + by < count]
    return lax.ppermute(value, axis, pairs)


def per_device(
    initial_head, conductivity, source_rate, storage_term, bed_conduct, row_cells, row_reach,
    river_section, bed_depth, route_inverse, retention, chain_heads,
):
    layers, rows, width = initial_head.shape
    fields = (initial_head, conductivity, source_rate, storage_term)
    edge = f32(4, layers, HALO, width)
    planes = -(-4 * layers // GROUPS)
    tall = rows + 2 * HALO
    side = f32(planes, tall, LANES)
    row_total = row_cells.shape[1]
    reaches = river_section.shape[1]
    cells = row_cells[0]

    def scratch(*shape):
        return pltpu.VMEM(shape, jnp.float32)

    last, first, info = call(
        front,
        (edge, edge, f32(row_total, LANES)),
        10,
        scratch=(
            pltpu.VMEM((1, row_total), jnp.int32),
            scratch(1, reaches),
            scratch(1, reaches),
            scratch(8, reaches),
            pltpu.SMEM((1,), jnp.float32),
            pltpu.SMEM((1,), jnp.int32),
            pltpu.SemaphoreType.DMA((14,)),
        ),
        anywhere=True,
        mib=60,
    )(*fields, row_reach, river_section, bed_depth, route_inverse, retention, chain_heads)
    low = shifted(last, "gx", 1)
    high = shifted(first, "gx", -1)
    info = lax.all_to_all(info, AXES, split_axis=0, concat_axis=0, tiled=True)
    beds = call(pick_beds, f32(row_total, LANES), 2, micros=2)(cells, bed_conduct)
    last, first = call(pack_y, (side, side), 6)(*fields, low, high)
    left = shifted(last, "gy", 1)
    right = shifted(first, "gy", -1)
    pads = tall + 2 * TOP
    sent, heads = call(
        upper,
        (
            f32(row_total, LANES),
            f32(2, 2, SWEEPS + 1, pads, LANES),
        ),
        11,
        scratch=(
            scratch(7, 2, SWEEPS, tall, LANES),
            scratch(2, SWEEPS + 1, pads, LANES),
            scratch(2, row_total // 2, LANES),
        ),
        mib=16,
        micros=5,
    )(*fields, low, high, left, right, cells, beds, info)
    arrived = lax.all_to_all(sent, AXES, split_axis=0, concat_axis=0, tiled=True)
    head_field, routed = call(
        lower,
        (f32(layers, rows, width), f32(row_total, reaches)),
        11,
        scratch=(
            scratch(2, 2, layers, pads, LANES),
            scratch(7, 2, layers, tall, LANES),
            scratch(2, layers, pads, LANES),
        ),
        mib=16,
        micros=5,
    )(*fields, low, high, left, right, heads, row_reach, route_inverse[0])
    reach_flow = call(finish_flow, f32(1, reaches), 2)(arrived, routed)
    return (head_field, reach_flow)


def solution(mesh):
    placed = (
        P(None, "gx", "gy"),
        P(None, "gx", "gy"),
        P(None, "gx", "gy"),
        P(None, "gx", "gy"),
        P("gx", "gy"),
        P(AXES, None, None),
        P(AXES, None),
        P(AXES, None),
        P(AXES, None),
        P(AXES, None, None),
        P(AXES),
        P(AXES),
    )
    return jax.shard_map(
        per_device,
        mesh=mesh,
        in_specs=placed,
        out_specs=(P(None, "gx", "gy"), P(AXES, None)),
        check_vma=False,
    )
```

```python
import jax
import jax.numpy as jnp
from jax import lax
from jax.experimental import pallas as pl
from jax.experimental.pallas import tpu as pltpu
from jax.sharding import PartitionSpec as P

SWEEPS = 8
HALO = 8
LANES = 128
GROUPS = LANES // HALO
AXES = ("gx", "gy")
VMEM = pl.BlockSpec(memory_space=pltpu.VMEM)
ANY = pl.BlockSpec(memory_space=pl.ANY)
TOP, BOTTOM = HALO, 2 * HALO


def call(body, out, count, scratch=(), anywhere=False, mib=8, micros=1):
    return pl.pallas_call(
        body,
        out_shape=out,
        in_specs=[ANY if anywhere else VMEM] * count,
        out_specs=jax.tree.map(lambda _: VMEM, out),
        scratch_shapes=list(scratch),
        compiler_params=pltpu.CompilerParams(vmem_limit_bytes=mib * 1024 * 1024),
        cost_estimate=pl.CostEstimate(
            flops=0, transcendentals=0, bytes_accessed=micros * 3_000_000
        ),
    )


def f32(*shape):
    return jax.ShapeDtypeStruct(shape, jnp.float32)


def front(
    head, cond, source, storage, reach, section, depth, route, retention, heads,
    last_out, first_out, info_out,
    reach_here, section_here, depth_here, weight_here, retention_here, heads_here, sems,
):
    rows = head.shape[1]
    reaches = section.shape[1]
    edges = []
    for k, ref in enumerate((head, cond, source, storage)):
        edges.append((ref.at[:, rows - HALO :, :], last_out.at[k]))
        edges.append((ref.at[:, :HALO, :], first_out.at[k]))
    small = [
        (reach, reach_here),
        (section, section_here),
        (depth, depth_here),
        (route.at[0, reaches - 8 :, :], weight_here),
        (retention, retention_here),
        (heads, heads_here),
    ]
    copies = [pltpu.make_async_copy(a, b, sems.at[i]) for i, (a, b) in enumerate(small + edges)]
    for copy in copies:
        copy.start()
    for copy in copies[: len(small)]:
        copy.wait()
    carry = retention_here[0] * (1.0 - heads_here[0].astype(jnp.float32))
    sec = section_here[...]
    table = jnp.concatenate(
        [sec, sec - depth_here[...], weight_here[7:8, :], jnp.full((5, reaches), carry)], 0
    )
    count = reach.shape[1]
    for part in range(count // LANES):
        spots = jnp.broadcast_to(reach_here[:, part * LANES : (part + 1) * LANES], (8, LANES))
        picked = jnp.zeros((8, LANES), jnp.float32)
        for block in range(reaches // LANES):
            value = jnp.take_along_axis(
                table[:, block * LANES : (block + 1) * LANES],
                spots & (LANES - 1),
                axis=1,
                mode="promise_in_bounds",
            )
            picked = jnp.where(spots // LANES == block, value, picked)
        tall = jnp.concatenate([picked, jnp.zeros((LANES - 8, LANES), jnp.float32)], 0)
        info_out[part * LANES : (part + 1) * LANES, :] = jnp.transpose(tall)
    for copy in copies[len(small) :]:
        copy.wait()


def pack_y(head, cond, source, storage, low, high, last_out, first_out):
    layers, rows, width = head.shape
    lane = lax.broadcasted_iota(jnp.int32, (rows + 2 * HALO, LANES), 1)
    first_sum = [None] * last_out.shape[0]
    last_sum = [None] * last_out.shape[0]
    for k, ref in enumerate((head, cond, source, storage)):
        for l in range(layers):
            plane, group = divmod(k * layers + l, GROUPS)
            whole = jnp.concatenate([low[k, l], ref[l], high[k, l]], 0)
            mine = (lane >= group * HALO) & (lane < (group + 1) * HALO)
            first = pltpu.roll(whole, group * HALO, 1) if group else whole
            turn = (group + 1) * HALO % LANES
            last = pltpu.roll(whole, turn, 1) if turn else whole
            if first_sum[plane] is None:
                first_sum[plane], last_sum[plane] = first, last
            else:
                first_sum[plane] = jnp.where(mine, first, first_sum[plane])
                last_sum[plane] = jnp.where(mine, last, last_sum[plane])
    for plane in range(last_out.shape[0]):
        first_out[plane] = first_sum[plane]
        last_out[plane] = last_sum[plane]


def select_cells(cells_ref, table, finish):
    for b in range(cells_ref.shape[0] // 8):
        cells = cells_ref[b * 8 : (b + 1) * 8, :]
        column, line = cells & (LANES - 1), cells // LANES
        found = jnp.zeros((8, LANES), jnp.float32)
        for r, spread in enumerate(table):
            value = jnp.take_along_axis(spread, column, axis=1, mode="promise_in_bounds")
            found = jnp.where(line == r, value, found)
        finish(b, found)


def spread_rows(table):
    return [jnp.broadcast_to(table[r : r + 1, :], (8, LANES)) for r in range(table.shape[0])]


def pick_beds(cells, bed, out):
    def finish(b, value):
        out[b * 8 : (b + 1) * 8, :] = value

    select_cells(cells, spread_rows(bed[...]), finish)


def extended(fields, halos, k, l):
    low, high, left, right = halos
    layers, rows, width = fields[k].shape
    lane = lax.broadcasted_iota(jnp.int32, (rows + 2 * HALO, LANES), 1)
    plane, group = divmod(k * layers + l, GROUPS)
    whole = jnp.concatenate([low[k, l], fields[k][l], high[k, l]], 0)
    after = right[plane]
    if group:
        after = pltpu.roll(after, LANES - group * HALO, 1)
    ahead = left[plane]
    turn = (LANES - HALO - group * HALO) % LANES
    if turn:
        ahead = pltpu.roll(ahead, turn, 1)
    side = jnp.where(lane < HALO, after, jnp.where(lane >= LANES - HALO, ahead, 0.0))
    return whole, side


def beside(pair):
    lane = lax.broadcasted_iota(jnp.int32, pair[0].shape, 1)
    ahead = [pltpu.roll(one, LANES - 1, 1) for one in pair]
    behind = [pltpu.roll(one, 1, 1) for one in pair]
    east = [jnp.where(lane == LANES - 1, ahead[1 - t], ahead[t]) for t in range(2)]
    west = [jnp.where(lane == 0, behind[1 - t], behind[t]) for t in range(2)]
    return east, west


def grid_mask(rows):
    row = lax.broadcasted_iota(jnp.int32, (rows, LANES), 0)
    lane = lax.broadcasted_iota(jnp.int32, (rows, LANES), 1)
    at_x, at_y = lax.axis_index("gx"), lax.axis_index("gy")
    first_row = jnp.where(at_x == 0, HALO, 0)
    last_row = jnp.where(at_x == lax.axis_size("gx") - 1, rows - HALO, rows)
    after = jnp.where(at_y == lax.axis_size("gy") - 1, 0, HALO)
    ahead = jnp.where(at_y == 0, LANES, LANES - HALO)
    tall = (row >= first_row) & (row < last_row)
    return [tall, tall & ((lane < after) | (lane >= ahead))]


def set_conduct(fields, halos, mask, conds, l, slot):
    rows = conds.shape[2]
    for t, value in enumerate(extended(fields, halos, 1, l)):
        conds[t, slot, TOP : rows - TOP, :] = jnp.where(mask[t], value, 0.0)
        conds[t, slot, :TOP, :] = jnp.zeros((TOP, LANES), jnp.float32)
        conds[t, slot, rows - TOP :, :] = jnp.zeros((TOP, LANES), jnp.float32)


def set_coefs(fields, halos, conds, slots, coef, l, at):
    rows = conds.shape[2]
    above, here, below = slots
    mids = [conds[t, here, TOP : rows - TOP, :] for t in range(2)]
    east, west = beside(mids)
    storage = extended(fields, halos, 3, l)
    source = extended(fields, halos, 2, l)
    for t in range(2):
        mid = mids[t]
        inside = mid > 0.0

        def face(near):
            return jnp.where(inside & (near > 0.0), 0.5 * (mid + near), 0.0)

        faces = [
            face(east[t]),
            face(west[t]),
            face(conds[t, here, TOP + 1 : rows - TOP + 1, :]),
            face(conds[t, here, TOP - 1 : rows - TOP - 1, :]),
            None if above is None else 0.5 * (mid + conds[t, above, TOP : rows - TOP, :]),
            None if below is None else 0.5 * (mid + conds[t, below, TOP : rows - TOP, :]),
        ]
        total = storage[t]
        for one in faces:
            if one is not None:
                total = total + one
        inverse = jnp.where(inside, 1.0 / jnp.where(inside, total, 1.0), 0.0)
        for k, one in enumerate(faces):
            if one is not None:
                coef[k, t, at] = one * inverse
        coef[6, t, at] = source[t] * inverse


def sweep(place, coef_of, time, first, last, top, only_main, store):
    for start in range(BOTTOM if only_main else TOP, top - (BOTTOM if only_main else TOP), 8):
        span = slice(start, start + 8)
        mids = {}
        for l in range(max(first - 1, 0), last + 2):
            if place(time, l) is not None:
                ref, at = place(time, l)
                mids[l] = [
                    ref[(*at, t, l, span, slice(None))] for t in range(2)
                ]
        for l in range(first, last + 1):
            ref, at = place(time, l)
            east, west = beside(mids[l])
            coef, c = coef_of(l)
            for t in range(1 if only_main else 2):
                rows = slice(start - TOP, start - TOP + 8)
                out = coef[6, t, c, rows, :] + coef[0, t, c, rows, :] * east[t]
                out = out + coef[1, t, c, rows, :] * west[t]
                out = out + coef[2, t, c, rows, :] * ref[(*at, t, l, slice(start + 1, start + 9), slice(None))]
                out = out + coef[3, t, c, rows, :] * ref[(*at, t, l, slice(start - 1, start + 7), slice(None))]
                if l - 1 in mids:
                    out = out + coef[4, t, c, rows, :] * mids[l - 1][t]
                if l + 1 in mids:
                    out = out + coef[5, t, c, rows, :] * mids[l + 1][t]
                store(l, t, start, out)


def set_heads(fields, halos, heads, l):
    rows = heads.shape[3]
    for t, value in enumerate(extended(fields, halos, 0, l)):
        heads[0, t, l, TOP : rows - TOP, :] = value
        for parity in range(2):
            heads[parity, t, l, :TOP, :] = jnp.zeros((TOP, LANES), jnp.float32)
            heads[parity, t, l, rows - TOP :, :] = jnp.zeros((TOP, LANES), jnp.float32)


def upper(
    head, cond, source, storage, low, high, left, right, cells, beds, info,
    send_out, heads, coef, conds, weights,
):
    fields, halos = (head, cond, source, storage), (low, high, left, right)
    layers, rows, width = head.shape
    peers = cells.shape[0] // 2
    mask = grid_mask(rows + 2 * HALO)
    for l in range(SWEEPS + 1):
        set_heads(fields, halos, heads, l)
        set_conduct(fields, halos, mask, conds, l, l)
    for l in range(SWEEPS):
        set_coefs(fields, halos, conds, (l - 1 if l else None, l, l + 1), coef, l, l)

    sub = lax.broadcasted_iota(jnp.int32, (peers, LANES), 0)
    lane = lax.broadcasted_iota(jnp.int32, (peers, LANES), 1)
    carry_column = info[pl.ds(0, peers, stride=2), :][:, 3:4]
    carry_row = jnp.sum(jnp.where(sub == lane, carry_column, 0.0), 0, keepdims=True)
    product = jnp.where(lane > sub, carry_row, 1.0)
    step = 1
    while step < LANES:
        product = product * jnp.where(lane >= step, pltpu.roll(product, step, 1), 1.0)
        step *= 2
    product = jnp.where(lane > sub, product, 0.0)
    for c in range(2):
        weights[c] = product * info[pl.ds(c, peers, stride=2), :][:, 2:3]

    for time in range(SWEEPS):

        def store(l, t, start, value):
            heads[(time + 1) % 2, t, l, start : start + 8, :] = value

        sweep(
            lambda when, l: (heads, (when % 2,)),
            lambda l: (coef, l),
            time, 0, SWEEPS - 1 - time, heads.shape[3], time == SWEEPS - 1, store,
        )

    table = heads[SWEEPS % 2, 0, 0, BOTTOM : BOTTOM + rows, :]
    leaks = []

    def finish(b, value):
        span = pl.ds(b * 8, 8)
        detail = info[span, :]
        leak = beds[span, :] * (jnp.maximum(value, detail[:, 1:2]) - detail[:, 0:1])
        leaks.append(jnp.sum(leak, 1, keepdims=True))

    select_cells(cells, spread_rows(table), finish)
    row_leak = jnp.concatenate(leaks, 0)
    lane2 = lax.broadcasted_iota(jnp.int32, (2 * peers, LANES), 1)
    send_out[...] = jnp.where(lane2 == 0, row_leak, 0.0)
    flow = jnp.zeros((peers, LANES), jnp.float32)
    for c in range(2):
        flow = flow + weights[c] * send_out[pl.ds(c, peers, stride=2), :][:, 0:1]
    flow = jnp.sum(flow, 0, keepdims=True)
    column = jnp.sum(jnp.where(sub == lane, flow, 0.0), 1, keepdims=True)
    even = send_out[pl.ds(0, peers, stride=2), :]
    send_out[pl.ds(0, peers, stride=2), :] = jnp.where(lane == 1, column, even)


def lower(
    head, cond, source, storage, low, high, left, right, heads, reach, route,
    field_out, routed_out, mine, coef, conds,
):
    fields, halos = (head, cond, source, storage), (low, high, left, right)
    layers, rows, width = head.shape
    mask = grid_mask(rows + 2 * HALO)
    for l in range(SWEEPS + 1, layers):
        set_heads(fields, halos, mine, l)
    for l in range(1, SWEEPS + 1):
        for t in range(2):
            for parity in range(2):
                mine[parity, t, l, :TOP, :] = jnp.zeros((TOP, LANES), jnp.float32)
                mine[parity, t, l, mine.shape[3] - TOP :, :] = jnp.zeros((TOP, LANES), jnp.float32)
    for l in range(layers):
        set_conduct(fields, halos, mask, conds, l, l)
    for l in range(1, layers):
        set_coefs(
            fields, halos, conds, (l - 1, l, l + 1 if l + 1 < layers else None), coef, l, l
        )

    def place(when, l):
        if l >= layers:
            return None
        return (heads if l <= SWEEPS and when <= SWEEPS - l else mine), (when % 2,)

    for time in range(SWEEPS):
        final = time == SWEEPS - 1

        def store(l, t, start, value):
            if final:
                field_out[l, start - BOTTOM : start - BOTTOM + 8, :] = value
            else:
                mine[(time + 1) % 2, t, l, start : start + 8, :] = value

        sweep(
            place,
            lambda l: (coef, l),
            time, SWEEPS - time, layers - 1, heads.shape[3], final, store,
        )
    field_out[0] = heads[SWEEPS % 2, 0, 0, BOTTOM : BOTTOM + rows, :]
    count, reaches = routed_out.shape
    line = lax.broadcasted_iota(jnp.int32, (reaches, count), 0)
    routed_out[...] = lax.dot_general(
        (line == reach[...]).astype(jnp.float32),
        route[...],
        (((0,), (1,)), ((), ())),
        precision=lax.Precision.HIGHEST,
        preferred_element_type=jnp.float32,
    )


def finish_flow(arrived, routed, out):
    parts = arrived[...]
    flow = jnp.sum(parts[:, 0:1] * routed[...], 0, keepdims=True)
    inflow = jnp.sum(parts[:, 1:2], 0, keepdims=True)
    out[...] = flow + inflow


def shifted(value, axis, by):
    count = lax.axis_size(axis)
    return lax.ppermute(value, axis, [(i, (i + by) % count) for i in range(count)])


def per_device(
    initial_head, conductivity, source_rate, storage_term, bed_conduct, row_cells, row_reach,
    river_section, bed_depth, route_inverse, retention, chain_heads,
):
    layers, rows, width = initial_head.shape
    fields = (initial_head, conductivity, source_rate, storage_term)
    edge = f32(4, layers, HALO, width)
    planes = -(-4 * layers // GROUPS)
    tall = rows + 2 * HALO
    side = f32(planes, tall, LANES)
    row_total = row_cells.shape[1]
    reaches = river_section.shape[1]
    cells = row_cells[0]

    def scratch(*shape):
        return pltpu.VMEM(shape, jnp.float32)

    last, first, info = call(
        front,
        (edge, edge, f32(row_total, LANES)),
        10,
        scratch=(
            pltpu.VMEM((1, row_total), jnp.int32),
            scratch(1, reaches),
            scratch(1, reaches),
            scratch(8, reaches),
            pltpu.SMEM((1,), jnp.float32),
            pltpu.SMEM((1,), jnp.int32),
            pltpu.SemaphoreType.DMA((14,)),
        ),
        anywhere=True,
        mib=60,
    )(*fields, row_reach, river_section, bed_depth, route_inverse, retention, chain_heads)
    low = shifted(last, "gx", 1)
    high = shifted(first, "gx", -1)
    info = lax.all_to_all(info, AXES, split_axis=0, concat_axis=0, tiled=True)
    beds = call(pick_beds, f32(row_total, LANES), 2, micros=2)(cells, bed_conduct)
    last, first = call(pack_y, (side, side), 6)(*fields, low, high)
    left = shifted(last, "gy", 1)
    right = shifted(first, "gy", -1)
    pads = tall + 2 * TOP
    sent, heads = call(
        upper,
        (
            f32(row_total, LANES),
            f32(2, 2, SWEEPS + 1, pads, LANES),
        ),
        11,
        scratch=(
            scratch(7, 2, SWEEPS, tall, LANES),
            scratch(2, SWEEPS + 1, pads, LANES),
            scratch(2, row_total // 2, LANES),
        ),
        mib=16,
        micros=5,
    )(*fields, low, high, left, right, cells, beds, info)
    arrived = lax.all_to_all(sent, AXES, split_axis=0, concat_axis=0, tiled=True)
    head_field, routed = call(
        lower,
        (f32(layers, rows, width), f32(row_total, reaches)),
        11,
        scratch=(
            scratch(2, 2, layers, pads, LANES),
            scratch(7, 2, layers, tall, LANES),
            scratch(2, layers, pads, LANES),
        ),
        mib=16,
        micros=5,
    )(*fields, low, high, left, right, heads, row_reach, route_inverse[0])
    reach_flow = call(finish_flow, f32(1, reaches), 2)(arrived, routed)
    return (head_field, reach_flow)


def solution(mesh):
    placed = (
        P(None, "gx", "gy"),
        P(None, "gx", "gy"),
        P(None, "gx", "gy"),
        P(None, "gx", "gy"),
        P("gx", "gy"),
        P(AXES, None, None),
        P(AXES, None),
        P(AXES, None),
        P(AXES, None),
        P(AXES, None, None),
        P(AXES),
        P(AXES),
    )
    return jax.shard_map(
        per_device,
        mesh=mesh,
        in_specs=placed,
        out_specs=(P(None, "gx", "gy"), P(AXES, None)),
        check_vma=False,
    )
```

```python
import functools

import jax
import jax.numpy as jnp
from jax import lax
from jax.experimental import pallas as pl
from jax.experimental.pallas import tpu as pltpu
from jax.sharding import PartitionSpec as P

SWEEPS = 8
HALO = 8
LANES = 128
GROUPS = LANES // HALO
AXES = ("gx", "gy")
VMEM = pl.BlockSpec(memory_space=pltpu.VMEM)
ANY = pl.BlockSpec(memory_space=pl.ANY)
TOP, BOTTOM = HALO, 2 * HALO


def call(body, out, count, scratch=(), anywhere=False, mib=8, micros=1):
    return pl.pallas_call(
        body,
        out_shape=out,
        in_specs=[ANY if anywhere else VMEM] * count,
        out_specs=jax.tree.map(lambda _: VMEM, out),
        scratch_shapes=list(scratch),
        compiler_params=pltpu.CompilerParams(vmem_limit_bytes=mib * 1024 * 1024),
        cost_estimate=pl.CostEstimate(
            flops=0, transcendentals=0, bytes_accessed=micros * 3_000_000
        ),
    )


def f32(*shape):
    return jax.ShapeDtypeStruct(shape, jnp.float32)


def front(
    head, cond, source, storage, reach, section, depth, route, retention, heads,
    last_out, first_out, info_out,
    reach_here, section_here, depth_here, weight_here, retention_here, heads_here, sems,
):
    rows = head.shape[1]
    reaches = section.shape[1]
    edges = []
    for k, ref in enumerate((head, cond, source, storage)):
        edges.append((ref.at[:, rows - HALO :, :], last_out.at[k]))
        edges.append((ref.at[:, :HALO, :], first_out.at[k]))
    small = [
        (reach, reach_here),
        (section, section_here),
        (depth, depth_here),
        (route.at[0, reaches - 8 :, :], weight_here),
        (retention, retention_here),
        (heads, heads_here),
    ]
    copies = [pltpu.make_async_copy(a, b, sems.at[i]) for i, (a, b) in enumerate(small + edges)]
    for copy in copies:
        copy.start()
    for copy in copies[: len(small)]:
        copy.wait()
    carry = retention_here[0] * (1.0 - heads_here[0].astype(jnp.float32))
    sec = section_here[...]
    table = jnp.concatenate(
        [sec, sec - depth_here[...], weight_here[7:8, :], jnp.full((5, reaches), carry)], 0
    )
    count = reach.shape[1]
    for part in range(count // LANES):
        spots = jnp.broadcast_to(reach_here[:, part * LANES : (part + 1) * LANES], (8, LANES))
        picked = jnp.zeros((8, LANES), jnp.float32)
        for block in range(reaches // LANES):
            value = jnp.take_along_axis(
                table[:, block * LANES : (block + 1) * LANES],
                spots & (LANES - 1),
                axis=1,
                mode="promise_in_bounds",
            )
            picked = jnp.where(spots // LANES == block, value, picked)
        tall = jnp.concatenate([picked, jnp.zeros((LANES - 8, LANES), jnp.float32)], 0)
        info_out[part * LANES : (part + 1) * LANES, :] = jnp.transpose(tall)
    for copy in copies[len(small) :]:
        copy.wait()


def pack_y(head, cond, source, storage, low, high, last_out, first_out):
    layers, rows, width = head.shape
    lane = lax.broadcasted_iota(jnp.int32, (rows + 2 * HALO, LANES), 1)
    first_sum = [None] * last_out.shape[0]
    last_sum = [None] * last_out.shape[0]
    for k, ref in enumerate((head, cond, source, storage)):
        for l in range(layers):
            plane, group = divmod(k * layers + l, GROUPS)
            whole = jnp.concatenate([low[k, l], ref[l], high[k, l]], 0)
            mine = (lane >= group * HALO) & (lane < (group + 1) * HALO)
            first = pltpu.roll(whole, group * HALO, 1) if group else whole
            turn = (group + 1) * HALO % LANES
            last = pltpu.roll(whole, turn, 1) if turn else whole
            if first_sum[plane] is None:
                first_sum[plane], last_sum[plane] = first, last
            else:
                first_sum[plane] = jnp.where(mine, first, first_sum[plane])
                last_sum[plane] = jnp.where(mine, last, last_sum[plane])
    for plane in range(last_out.shape[0]):
        first_out[plane] = first_sum[plane]
        last_out[plane] = last_sum[plane]


def select_cells(cells_ref, table, finish):
    half = cells_ref.shape[0] // 16
    for b in range(2 * half):
        c, g = divmod(b, half)
        cells = cells_ref[pl.ds(g * 16 + c, 8, stride=2), :]
        column, line = cells & (LANES - 1), cells // LANES
        found = jnp.zeros((8, LANES), jnp.float32)
        for r, spread in enumerate(table):
            value = jnp.take_along_axis(spread, column, axis=1, mode="promise_in_bounds")
            found = jnp.where(line == r, value, found)
        finish(slice(b * 8, (b + 1) * 8), found)


def spread_rows(table):
    return [jnp.broadcast_to(table[r : r + 1, :], (8, LANES)) for r in range(table.shape[0])]


def tall_row(fields, low, high, k, l):
    return jnp.concatenate([low[k, l], fields[k][l], high[k, l]], 0)


def turned(value, by):
    return pltpu.roll(value, by % LANES, 1) if by % LANES else value


def side_tiles(fields, low, high, left, right):
    layers = fields[0].shape[0]

    def get(k, l):
        plane, group = divmod(k * layers + l, GROUPS)
        whole = tall_row(fields, low, high, k, l)
        lane = lax.broadcasted_iota(jnp.int32, whole.shape, 1)
        after = turned(right[plane], -group * HALO)
        ahead = turned(left[plane], LANES - HALO - group * HALO)
        side = jnp.where(lane < HALO, after, jnp.where(lane >= LANES - HALO, ahead, 0.0))
        return [whole, side]

    return get


def strip_tiles(strips, left, right, layers):
    def get(k, l):
        plane, group = divmod(k * layers + l, GROUPS)
        lane = lax.broadcasted_iota(jnp.int32, left.shape[1:], 1)
        after = turned(right[plane], 2 * HALO - group * HALO)
        ahead = turned(left[plane], 3 * HALO - group * HALO)
        own = strips[k, l]
        inner = jnp.where(lane < 3 * HALO, after, ahead)
        return [jnp.where((lane >= 2 * HALO) & (lane < 4 * HALO), inner, own)]

    return get


def inside_rows(row):
    at_x = lax.axis_index("gx")
    first_row = jnp.where(at_x == 0, HALO, 0)
    last_row = jnp.where(at_x == lax.axis_size("gx") - 1, row.shape[0] - HALO, row.shape[0])
    return (row >= first_row) & (row < last_row)


def beside(tiles):
    lane = lax.broadcasted_iota(jnp.int32, tiles[0].shape, 1)
    ahead = [pltpu.roll(one, LANES - 1, 1) for one in tiles]
    behind = [pltpu.roll(one, 1, 1) for one in tiles]
    if len(tiles) == 1:
        return ahead, behind
    east = [jnp.where(lane == LANES - 1, ahead[1 - t], ahead[t]) for t in range(2)]
    west = [jnp.where(lane == 0, behind[1 - t], behind[t]) for t in range(2)]
    return east, west


def set_coefs(get, conds, coef, l, bottom):
    tiles, rows = conds.shape[0], conds.shape[2]
    span = slice(TOP, rows - TOP)
    east, west = beside([conds[t, l, span, :] for t in range(tiles)])
    storage, source = get(3, l), get(2, l)
    for t in range(tiles):
        mid = conds[t, l, span, :]
        inside = mid > 0.0

        def face(near):
            return jnp.where(inside & (near > 0.0), 0.5 * (mid + near), 0.0)

        faces = [
            face(east[t]),
            face(west[t]),
            face(conds[t, l, TOP + 1 : rows - TOP + 1, :]),
            face(conds[t, l, TOP - 1 : rows - TOP - 1, :]),
            0.5 * (mid + conds[t, l - 1, span, :]) if l else None,
            None if bottom else 0.5 * (mid + conds[t, l + 1, span, :]),
        ]
        total = storage[t]
        for one in faces:
            if one is not None:
                total = total + one
        inverse = jnp.where(inside, 1.0 / jnp.where(inside, total, 1.0), 0.0)
        for k, one in enumerate(faces):
            if one is not None:
                coef[k, t, l] = one * inverse
        coef[6, t, l] = source[t] * inverse


def relax(get, masks, heads, coef, conds, layers, cone, final):
    tiles, held, rows = heads.shape[1:4]
    edge = jnp.zeros((TOP, LANES), jnp.float32)
    for l in range(held):
        for t, value in enumerate(get(0, l)):
            heads[0, t, l, TOP : rows - TOP, :] = value
        for t, value in enumerate(get(1, l)):
            conds[t, l, TOP : rows - TOP, :] = jnp.where(masks[t], value, 0.0)
            for span in (slice(0, TOP), slice(rows - TOP, rows)):
                conds[t, l, span, :] = edge
                heads[0, t, l, span, :] = edge
                heads[1, t, l, span, :] = edge
    for l in range(held - 1 if cone else held):
        set_coefs(get, conds, coef, l, l + 1 == layers)
    for time in range(SWEEPS):
        last_sweep = time == SWEEPS - 1
        margin = BOTTOM if last_sweep else TOP
        many = SWEEPS - time if cone else layers
        old = time % 2
        for start in range(margin, rows - margin, 8):
            span = slice(start, start + 8)
            mids = [
                [heads[old, t, l, span, :] for t in range(tiles)]
                for l in range(min(many + 1, layers))
            ]
            for l in range(many):
                east, west = beside(mids[l])
                at = slice(start - TOP, start - TOP + 8)
                for t in range(1 if last_sweep else tiles):
                    out = coef[6, t, l, at, :] + coef[0, t, l, at, :] * east[t]
                    out = out + coef[1, t, l, at, :] * west[t]
                    out = out + coef[2, t, l, at, :] * heads[old, t, l, start + 1 : start + 9, :]
                    out = out + coef[3, t, l, at, :] * heads[old, t, l, start - 1 : start + 7, :]
                    if l:
                        out = out + coef[4, t, l, at, :] * mids[l - 1][t]
                    if l + 1 < layers:
                        out = out + coef[5, t, l, at, :] * mids[l + 1][t]
                    if last_sweep:
                        final(l, start - BOTTOM, out)
                    else:
                        heads[1 - old, t, l, span, :] = out


def inner(
    head, cond, source, storage, low, high, cells, bed,
    beds_out, top_out, strips_out, heads, coef, conds,
):
    fields = (head, cond, source, storage)
    layers, rows, width = head.shape
    tall = rows + 2 * HALO
    lane = lax.broadcasted_iota(jnp.int32, (tall, LANES), 1)
    for k in range(4):
        for l in range(SWEEPS + 1 if k < 2 else SWEEPS):
            whole = tall_row(fields, low, high, k, l)
            strip = jnp.where(lane < 2 * HALO, turned(whole, 2 * HALO), turned(whole, 4 * HALO))
            strips_out[k, l] = jnp.where(lane < 6 * HALO, strip, 0.0)

    def keep(span, value):
        beds_out[span, :] = value

    select_cells(cells, spread_rows(bed[...]), keep)

    def final(l, start, value):
        top_out[start : start + 8, :] = value

    inside = inside_rows(lax.broadcasted_iota(jnp.int32, (tall, LANES), 0))
    relax(
        lambda k, l: [tall_row(fields, low, high, k, l)], [inside],
        heads, coef, conds, layers, True, final,
    )


def edges(layers, strips, left, right, top, table, heads, coef, conds):
    tall = top.shape[0] + 2 * HALO
    lane = lax.broadcasted_iota(jnp.int32, (tall, LANES), 1)
    at_y = lax.axis_index("gy")
    first = (at_y == 0) & (lane >= 3 * HALO) & (lane < 4 * HALO)
    last = (at_y == lax.axis_size("gy") - 1) & (lane >= 2 * HALO) & (lane < 3 * HALO)
    inside = inside_rows(lax.broadcasted_iota(jnp.int32, (tall, LANES), 0))
    mask = inside & ~first & ~last & (lane < 6 * HALO)

    def final(l, start, value):
        span = slice(start, start + 8)
        column = lax.broadcasted_iota(jnp.int32, value.shape, 1)
        ends = jnp.where(column < HALO, turned(value, -4 * HALO), turned(value, -2 * HALO))
        table[span, :] = jnp.where(
            (column < HALO) | (column >= LANES - HALO), ends, top[span, :]
        )

    relax(
        strip_tiles(strips, left, right, layers), [mask],
        heads, coef, conds, layers, True, final,
    )


def leak_rows(table, cells, beds, info, send_out, weights, levels, leaks):
    peers = info.shape[0] // 2
    groups = peers // 8
    for c in range(2):
        for g in range(groups):
            detail = info[pl.ds(g * 16 + c, 8, stride=2), :]
            span = slice((c * groups + g) * 8, (c * groups + g + 1) * 8)
            for k in range(2):
                levels[k, span, :] = jnp.broadcast_to(detail[:, k : k + 1], (8, LANES))

    sub = lax.broadcasted_iota(jnp.int32, (peers, LANES), 0)
    lane = lax.broadcasted_iota(jnp.int32, (peers, LANES), 1)
    details = [info[pl.ds(c, peers, stride=2), :] for c in range(2)]
    carry_row = jnp.sum(jnp.where(sub == lane, details[0][:, 3:4], 0.0), 0, keepdims=True)
    product = jnp.where(lane > sub, carry_row, 1.0)
    step = 1
    while step < LANES:
        product = product * jnp.where(lane >= step, pltpu.roll(product, step, 1), 1.0)
        step *= 2
    product = jnp.where(lane > sub, product, 0.0)
    for c in range(2):
        weights[c] = product * details[c][:, 2:3]

    def leak(span, value):
        leaks[span, :] = beds[span, :] * (
            jnp.maximum(value, levels[1, span, :]) - levels[0, span, :]
        )

    select_cells(cells, spread_rows(table[...]), leak)
    eight = lax.broadcasted_iota(jnp.int32, (8, LANES), 1)
    flow = jnp.zeros((8, LANES), jnp.float32)
    sums = []
    for g in range(groups):
        span = slice(g * 8, (g + 1) * 8)
        row_leak = [
            jnp.sum(leaks[c * peers + g * 8 : c * peers + (g + 1) * 8, :], 1, keepdims=True)
            for c in range(2)
        ]
        for c in range(2):
            flow = flow + weights[c, span, :] * row_leak[c]
        sums.append(jnp.where(eight == 0, row_leak[0], row_leak[1]))
    flow = jnp.sum(flow, 0, keepdims=True)
    for g in range(groups):
        mine = lax.broadcasted_iota(jnp.int32, (8, LANES), 0) + g * 8 == eight
        column = jnp.sum(jnp.where(mine, flow, 0.0), 1, keepdims=True)
        send_out[g * 8 : (g + 1) * 8, :] = jnp.where(eight == 2, column, sums[g])


def everywhere(
    head, cond, source, storage, low, high, left, right, reach, route,
    field_out, routed_out, heads, coef, conds, lines,
):
    fields = (head, cond, source, storage)
    layers, rows, width = head.shape
    tall = rows + 2 * HALO
    lane = lax.broadcasted_iota(jnp.int32, (tall, LANES), 1)
    inside = inside_rows(lax.broadcasted_iota(jnp.int32, (tall, LANES), 0))
    at_y = lax.axis_index("gy")
    after = jnp.where(at_y == lax.axis_size("gy") - 1, 0, HALO)
    ahead = jnp.where(at_y == 0, LANES, LANES - HALO)

    def final(l, start, value):
        field_out[l, start : start + 8, :] = value

    relax(
        side_tiles(fields, low, high, left, right),
        [inside, inside & ((lane < after) | (lane >= ahead))],
        heads, coef, conds, layers, False, final,
    )
    count, reaches = routed_out.shape
    line = lax.broadcasted_iota(jnp.int32, (reaches, count), 0)
    routed = lax.dot_general(
        (line == reach[...]).astype(jnp.float32),
        route[...],
        (((0,), (1,)), ((), ())),
        precision=lax.Precision.HIGHEST,
        preferred_element_type=jnp.float32,
    )
    for part in range(reaches // LANES):
        lines[part] = routed[:, part * LANES : (part + 1) * LANES]
    for part in range(reaches // LANES):
        for c in range(2):
            routed_out[c * (count // 2) : (c + 1) * (count // 2), part * LANES : (part + 1) * LANES] = (
                lines[part, pl.ds(c, count // 2, stride=2), :]
            )


def finish_flow(arrived, routed, out):
    half = arrived.shape[0]
    parts = arrived[...]
    flow = parts[:, 0:1] * routed[:half, :] + parts[:, 1:2] * routed[half:, :]
    out[...] = jnp.sum(flow + parts[:, 2:3], 0, keepdims=True)


def shifted(value, axis, by):
    count = lax.axis_size(axis)
    return lax.ppermute(value, axis, [(i, (i + by) % count) for i in range(count)])


def per_device(
    initial_head, conductivity, source_rate, storage_term, bed_conduct, row_cells, row_reach,
    river_section, bed_depth, route_inverse, retention, chain_heads,
):
    layers, rows, width = initial_head.shape
    fields = (initial_head, conductivity, source_rate, storage_term)
    edge = f32(4, layers, HALO, width)
    planes = -(-4 * layers // GROUPS)
    tall = rows + 2 * HALO
    side = f32(planes, tall, LANES)
    row_total = row_cells.shape[1]
    reaches = river_section.shape[1]
    cells = row_cells[0]

    def scratch(*shape):
        return pltpu.VMEM(shape, jnp.float32)

    last, first, info = call(
        front,
        (edge, edge, f32(row_total, LANES)),
        10,
        scratch=(
            pltpu.VMEM((1, row_total), jnp.int32),
            scratch(1, reaches),
            scratch(1, reaches),
            scratch(8, reaches),
            pltpu.SMEM((1,), jnp.float32),
            pltpu.SMEM((1,), jnp.int32),
            pltpu.SemaphoreType.DMA((14,)),
        ),
        anywhere=True,
        mib=60,
    )(*fields, row_reach, river_section, bed_depth, route_inverse, retention, chain_heads)
    low = shifted(last, "gx", 1)
    high = shifted(first, "gx", -1)
    info = lax.all_to_all(info, AXES, split_axis=0, concat_axis=0, tiled=True)
    last, first = call(pack_y, (side, side), 6)(*fields, low, high)
    left = shifted(last, "gy", 1)
    right = shifted(first, "gy", -1)
    pads = tall + 2 * TOP
    held = SWEEPS + 1
    own = (
        scratch(2, 1, held, pads, LANES),
        scratch(7, 1, SWEEPS, tall, LANES),
        scratch(1, held, pads, LANES),
    )
    beds, top, strips = call(
        inner,
        (f32(row_total, LANES), f32(rows, width), f32(4, held, tall, LANES)),
        8,
        scratch=own,
        mib=16,
        micros=3,
    )(*fields, low, high, cells, bed_conduct)
    table = call(
        functools.partial(edges, layers), f32(rows, width), 4, scratch=own, mib=16, micros=2
    )(strips, left, right, top)
    sent = call(
        leak_rows,
        f32(row_total // 2, LANES),
        4,
        scratch=(
            scratch(2, row_total // 2, LANES),
            scratch(2, row_total, LANES),
            scratch(row_total, LANES),
        ),
        micros=3,
    )(table, cells, beds, info)
    arrived = lax.all_to_all(sent, AXES, split_axis=0, concat_axis=0, tiled=True)
    head_field, routed = call(
        everywhere,
        (f32(layers, rows, width), f32(row_total, reaches)),
        10,
        scratch=(
            scratch(2, 2, layers, pads, LANES),
            scratch(7, 2, layers, tall, LANES),
            scratch(2, layers, pads, LANES),
            scratch(reaches // LANES, row_total, LANES),
        ),
        mib=20,
        micros=5,
    )(*fields, low, high, left, right, row_reach, route_inverse[0])
    reach_flow = call(finish_flow, f32(1, reaches), 2)(arrived, routed)
    return (head_field, reach_flow)


def solution(mesh):
    placed = (
        P(None, "gx", "gy"),
        P(None, "gx", "gy"),
        P(None, "gx", "gy"),
        P(None, "gx", "gy"),
        P("gx", "gy"),
        P(AXES, None, None),
        P(AXES, None),
        P(AXES, None),
        P(AXES, None),
        P(AXES, None, None),
        P(AXES),
        P(AXES),
    )
    return jax.shard_map(
        per_device,
        mesh=mesh,
        in_specs=placed,
        out_specs=(P(None, "gx", "gy"), P(AXES, None)),
        check_vma=False,
    )
```

```python
import functools

import jax
import jax.numpy as jnp
from jax import lax
from jax.experimental import pallas as pl
from jax.experimental.pallas import tpu as pltpu
from jax.sharding import PartitionSpec as P

SWEEPS = 8
HALO = 8
LANES = 128
GROUPS = LANES // HALO
AXES = ("gx", "gy")
VMEM = pl.BlockSpec(memory_space=pltpu.VMEM)
ANY = pl.BlockSpec(memory_space=pl.ANY)
TOP, BOTTOM = HALO, 2 * HALO


def call(body, out, count, scratch=(), anywhere=False, mib=8, micros=1):
    return pl.pallas_call(
        body,
        out_shape=out,
        in_specs=[ANY if anywhere else VMEM] * count,
        out_specs=jax.tree.map(lambda _: VMEM, out),
        scratch_shapes=list(scratch),
        compiler_params=pltpu.CompilerParams(vmem_limit_bytes=mib * 1024 * 1024),
        cost_estimate=pl.CostEstimate(
            flops=0, transcendentals=0, bytes_accessed=micros * 3_000_000
        ),
    )


def f32(*shape):
    return jax.ShapeDtypeStruct(shape, jnp.float32)


def front(
    head, cond, source, storage, reach, section, depth, route, retention, heads,
    last_out, first_out, info_out,
    reach_here, section_here, depth_here, weight_here, retention_here, heads_here, sems,
):
    rows = head.shape[1]
    reaches = section.shape[1]
    edges = []
    for k, ref in enumerate((head, cond, source, storage)):
        edges.append((ref.at[:, rows - HALO :, :], last_out.at[k]))
        edges.append((ref.at[:, :HALO, :], first_out.at[k]))
    small = [
        (reach, reach_here),
        (section, section_here),
        (depth, depth_here),
        (route.at[0, reaches - 8 :, :], weight_here),
        (retention, retention_here),
        (heads, heads_here),
    ]
    copies = [pltpu.make_async_copy(a, b, sems.at[i]) for i, (a, b) in enumerate(small + edges)]
    for copy in copies:
        copy.start()
    for copy in copies[: len(small)]:
        copy.wait()
    carry = retention_here[0] * (1.0 - heads_here[0].astype(jnp.float32))
    sec = section_here[...]
    table = jnp.concatenate(
        [sec, sec - depth_here[...], weight_here[7:8, :], jnp.full((5, reaches), carry)], 0
    )
    count = reach.shape[1]
    for part in range(count // LANES):
        spots = jnp.broadcast_to(reach_here[:, part * LANES : (part + 1) * LANES], (8, LANES))
        picked = jnp.zeros((8, LANES), jnp.float32)
        for block in range(reaches // LANES):
            value = jnp.take_along_axis(
                table[:, block * LANES : (block + 1) * LANES],
                spots & (LANES - 1),
                axis=1,
                mode="promise_in_bounds",
            )
            picked = jnp.where(spots // LANES == block, value, picked)
        tall = jnp.concatenate([picked, jnp.zeros((LANES - 8, LANES), jnp.float32)], 0)
        info_out[part * LANES : (part + 1) * LANES, :] = jnp.transpose(tall)
    for copy in copies[len(small) :]:
        copy.wait()


def pack_y(head, cond, source, storage, low, high, even_out, odd_out):
    fields = (head, cond, source, storage)
    layers, rows, width = head.shape
    even_y = lax.axis_index("gy") % 2 == 0
    lane = lax.broadcasted_iota(jnp.int32, (rows + 2 * HALO, LANES), 1)
    first_sum = [None] * even_out.shape[0]
    last_sum = [None] * even_out.shape[0]
    for k in range(4):
        for l in range(layers):
            plane, group = divmod(k * layers + l, GROUPS)
            whole = tall_row(fields, (low, high), k, l)
            spread = turned(whole, group * HALO)
            if first_sum[plane] is None:
                first_sum[plane], last_sum[plane] = spread, spread
            else:
                first_sum[plane] = jnp.where(
                    lane // HALO == group, spread, first_sum[plane]
                )
                last_sum[plane] = jnp.where(
                    lane // HALO == (group - 1) % GROUPS, spread, last_sum[plane]
                )
    for plane in range(even_out.shape[0]):
        even_out[plane] = jnp.where(even_y, last_sum[plane], first_sum[plane])
        odd_out[plane] = jnp.where(even_y, first_sum[plane], last_sum[plane])


def select_cells(cells_ref, table, finish):
    half = cells_ref.shape[0] // 16
    for b in range(2 * half):
        c, g = divmod(b, half)
        cells = cells_ref[pl.ds(g * 16 + c, 8, stride=2), :]
        column, line = cells & (LANES - 1), cells // LANES
        found = jnp.zeros((8, LANES), jnp.float32)
        for r, spread in enumerate(table):
            value = jnp.take_along_axis(spread, column, axis=1, mode="promise_in_bounds")
            found = jnp.where(line == r, value, found)
        finish(slice(b * 8, (b + 1) * 8), found)


def spread_rows(table):
    return [jnp.broadcast_to(table[r : r + 1, :], (8, LANES)) for r in range(table.shape[0])]


def tall_row(fields, beside_x, k, l):
    low, high = beside_x
    return jnp.concatenate([low[k, l], fields[k][l], high[k, l]], 0)


def settle(one, other, sides):
    even = lax.axis_index("gy") % 2 == 0
    for plane in range(sides.shape[1]):
        sides[0, plane] = jnp.where(even, other[plane], one[plane])
        sides[1, plane] = jnp.where(even, one[plane], other[plane])


def turned(value, by):
    return pltpu.roll(value, by % LANES, 1) if by % LANES else value


def side_tiles(fields, beside_x, sides):
    layers = fields[0].shape[0]

    def get(k, l):
        plane, group = divmod(k * layers + l, GROUPS)
        whole = tall_row(fields, beside_x, k, l)
        lane = lax.broadcasted_iota(jnp.int32, whole.shape, 1)
        both = jnp.where(lane // HALO == group, sides[1, plane], sides[0, plane])
        near = (lane < HALO) | (lane >= LANES - HALO)
        side = jnp.where(near, turned(both, -group * HALO), 0.0)
        return [whole, side]

    return get


def strip_tiles(strips, sides, layers):
    def get(k, l):
        plane, group = divmod(k * layers + l, GROUPS)
        lane = lax.broadcasted_iota(jnp.int32, sides.shape[2:], 1)
        after = turned(sides[1, plane], 2 * HALO - group * HALO)
        ahead = turned(sides[0, plane], 3 * HALO - (group - 1) % GROUPS * HALO)
        own = strips[k, l]
        inner = jnp.where(lane < 3 * HALO, after, ahead)
        return [jnp.where((lane >= 2 * HALO) & (lane < 4 * HALO), inner, own)]

    return get


def inside_rows(row):
    at_x = lax.axis_index("gx")
    first_row = jnp.where(at_x == 0, HALO, 0)
    last_row = jnp.where(at_x == lax.axis_size("gx") - 1, row.shape[0] - HALO, row.shape[0])
    return (row >= first_row) & (row < last_row)


def beside(tiles):
    lane = lax.broadcasted_iota(jnp.int32, tiles[0].shape, 1)
    ahead = [pltpu.roll(one, LANES - 1, 1) for one in tiles]
    behind = [pltpu.roll(one, 1, 1) for one in tiles]
    if len(tiles) == 1:
        return ahead, behind
    east = [jnp.where(lane == LANES - 1, ahead[1 - t], ahead[t]) for t in range(2)]
    west = [jnp.where(lane == 0, behind[1 - t], behind[t]) for t in range(2)]
    return east, west


def set_coefs(get, conds, coef, l, bottom):
    tiles, rows = conds.shape[0], conds.shape[2]
    span = slice(TOP, rows - TOP)
    east, west = beside([conds[t, l, span, :] for t in range(tiles)])
    storage, source = get(3, l), get(2, l)
    for t in range(tiles):
        mid = conds[t, l, span, :]
        inside = mid > 0.0

        def face(near):
            return jnp.where(inside & (near > 0.0), 0.5 * (mid + near), 0.0)

        faces = [
            face(east[t]),
            face(west[t]),
            face(conds[t, l, TOP + 1 : rows - TOP + 1, :]),
            face(conds[t, l, TOP - 1 : rows - TOP - 1, :]),
            0.5 * (mid + conds[t, l - 1, span, :]) if l else None,
            None if bottom else 0.5 * (mid + conds[t, l + 1, span, :]),
        ]
        total = storage[t]
        for one in faces:
            if one is not None:
                total = total + one
        inverse = jnp.where(inside, 1.0 / jnp.where(inside, total, 1.0), 0.0)
        for k, one in enumerate(faces):
            if one is not None:
                coef[k, t, l] = one * inverse
        coef[6, t, l] = source[t] * inverse


def relax(get, masks, heads, coef, conds, layers, cone, final):
    tiles, held, rows = heads.shape[1:4]
    edge = jnp.zeros((TOP, LANES), jnp.float32)
    for l in range(held):
        for t, value in enumerate(get(0, l)):
            heads[0, t, l, TOP : rows - TOP, :] = value
        for t, value in enumerate(get(1, l)):
            conds[t, l, TOP : rows - TOP, :] = jnp.where(masks[t], value, 0.0)
            for span in (slice(0, TOP), slice(rows - TOP, rows)):
                conds[t, l, span, :] = edge
                heads[0, t, l, span, :] = edge
                heads[1, t, l, span, :] = edge
    for l in range(held - 1 if cone else held):
        set_coefs(get, conds, coef, l, l + 1 == layers)
    for time in range(SWEEPS):
        last_sweep = time == SWEEPS - 1
        margin = BOTTOM if last_sweep else TOP
        many = SWEEPS - time if cone else layers
        old = time % 2
        for start in range(margin, rows - margin, 8):
            span = slice(start, start + 8)
            mids = [
                [heads[old, t, l, span, :] for t in range(tiles)]
                for l in range(min(many + 1, layers))
            ]
            for l in range(many):
                east, west = beside(mids[l])
                at = slice(start - TOP, start - TOP + 8)
                for t in range(1 if last_sweep else tiles):
                    out = coef[6, t, l, at, :] + coef[0, t, l, at, :] * east[t]
                    out = out + coef[1, t, l, at, :] * west[t]
                    out = out + coef[2, t, l, at, :] * heads[old, t, l, start + 1 : start + 9, :]
                    out = out + coef[3, t, l, at, :] * heads[old, t, l, start - 1 : start + 7, :]
                    if l:
                        out = out + coef[4, t, l, at, :] * mids[l - 1][t]
                    if l + 1 < layers:
                        out = out + coef[5, t, l, at, :] * mids[l + 1][t]
                    if last_sweep:
                        final(l, start - BOTTOM, out)
                    else:
                        heads[1 - old, t, l, span, :] = out


def inner(
    head, cond, source, storage, low, high, cells, bed,
    beds_out, top_out, strips_out, heads, coef, conds,
):
    fields = (head, cond, source, storage)
    beside_x = (low, high)
    layers, rows, width = head.shape
    tall = rows + 2 * HALO
    lane = lax.broadcasted_iota(jnp.int32, (tall, LANES), 1)
    for k in range(4):
        for l in range(SWEEPS + 1 if k < 2 else SWEEPS):
            whole = tall_row(fields, beside_x, k, l)
            strip = jnp.where(lane < 2 * HALO, turned(whole, 2 * HALO), turned(whole, 4 * HALO))
            strips_out[k, l] = jnp.where(lane < 6 * HALO, strip, 0.0)

    def keep(span, value):
        beds_out[span, :] = value

    select_cells(cells, spread_rows(bed[...]), keep)

    def final(l, start, value):
        top_out[start : start + 8, :] = value

    inside = inside_rows(lax.broadcasted_iota(jnp.int32, (tall, LANES), 0))
    relax(
        lambda k, l: [tall_row(fields, beside_x, k, l)], [inside],
        heads, coef, conds, layers, True, final,
    )


def edges(layers, strips, other_y, one_y, top, table, heads, coef, conds, sides):
    settle(one_y, other_y, sides)
    tall = top.shape[0] + 2 * HALO
    lane = lax.broadcasted_iota(jnp.int32, (tall, LANES), 1)
    at_y = lax.axis_index("gy")
    first = (at_y == 0) & (lane >= 3 * HALO) & (lane < 4 * HALO)
    last = (at_y == lax.axis_size("gy") - 1) & (lane >= 2 * HALO) & (lane < 3 * HALO)
    inside = inside_rows(lax.broadcasted_iota(jnp.int32, (tall, LANES), 0))
    mask = inside & ~first & ~last & (lane < 6 * HALO)

    def final(l, start, value):
        span = slice(start, start + 8)
        column = lax.broadcasted_iota(jnp.int32, value.shape, 1)
        ends = jnp.where(column < HALO, turned(value, -4 * HALO), turned(value, -2 * HALO))
        table[span, :] = jnp.where(
            (column < HALO) | (column >= LANES - HALO), ends, top[span, :]
        )

    relax(
        strip_tiles(strips, sides, layers), [mask],
        heads, coef, conds, layers, True, final,
    )


def leak_rows(table, cells, beds, info, send_out, weights, levels, leaks):
    peers = info.shape[0] // 2
    groups = peers // 8
    for c in range(2):
        for g in range(groups):
            detail = info[pl.ds(g * 16 + c, 8, stride=2), :]
            span = slice((c * groups + g) * 8, (c * groups + g + 1) * 8)
            for k in range(2):
                levels[k, span, :] = jnp.broadcast_to(detail[:, k : k + 1], (8, LANES))

    def running(value, lane, length):
        step = 1
        while step < length:
            value = value * jnp.where(lane % length >= step, pltpu.roll(value, step, 1), 1.0)
            step *= 2
        return value

    sub = lax.broadcasted_iota(jnp.int32, (peers, LANES), 0)
    lane = lax.broadcasted_iota(jnp.int32, (peers, LANES), 1)
    details = [info[pl.ds(c, peers, stride=2), :] for c in range(2)]
    carry_row = jnp.sum(jnp.where(sub == lane, details[0][:, 3:4], 0.0), 0, keepdims=True)
    sub, lane = sub[:8], lane[:8]
    within = running(jnp.where(lane % 8 > sub, carry_row, 1.0), lane, 8)
    own = jnp.where(lane % 8 > sub, within, 0.0)
    block = lax.broadcasted_iota(jnp.int32, (groups, LANES), 0)
    wide = lax.broadcasted_iota(jnp.int32, (groups, LANES), 1)
    beyond = running(jnp.where(wide > block * 8 + 7, carry_row, 1.0), wide, LANES)
    for g in range(groups):
        through = within[:, g * 8 + 7 : g * 8 + 8] * beyond[g : g + 1, :]
        product = jnp.where(lane // 8 == g, own, jnp.where(lane // 8 > g, through, 0.0))
        for c in range(2):
            weights[c, g * 8 : (g + 1) * 8, :] = product * details[c][g * 8 : (g + 1) * 8, 2:3]

    def leak(span, value):
        leaks[span, :] = beds[span, :] * (
            jnp.maximum(value, levels[1, span, :]) - levels[0, span, :]
        )

    select_cells(cells, spread_rows(table[...]), leak)
    eight = lax.broadcasted_iota(jnp.int32, (8, LANES), 1)
    flow = jnp.zeros((8, LANES), jnp.float32)
    sums = []
    for g in range(groups):
        span = slice(g * 8, (g + 1) * 8)
        row_leak = [
            jnp.sum(leaks[c * peers + g * 8 : c * peers + (g + 1) * 8, :], 1, keepdims=True)
            for c in range(2)
        ]
        for c in range(2):
            flow = flow + weights[c, span, :] * row_leak[c]
        sums.append(jnp.where(eight == 0, row_leak[0], row_leak[1]))
    flow = jnp.sum(flow, 0, keepdims=True)
    for g in range(groups):
        mine = lax.broadcasted_iota(jnp.int32, (8, LANES), 0) + g * 8 == eight
        column = jnp.sum(jnp.where(mine, flow, 0.0), 1, keepdims=True)
        send_out[g * 8 : (g + 1) * 8, :] = jnp.where(eight == 2, column, sums[g])


def everywhere(
    head, cond, source, storage, low, high, other_y, one_y, reach, route,
    field_out, routed_out, heads, coef, conds, lines, sides,
):
    fields = (head, cond, source, storage)
    beside_x = (low, high)
    settle(one_y, other_y, sides)
    layers, rows, width = head.shape
    tall = rows + 2 * HALO
    lane = lax.broadcasted_iota(jnp.int32, (tall, LANES), 1)
    inside = inside_rows(lax.broadcasted_iota(jnp.int32, (tall, LANES), 0))
    at_y = lax.axis_index("gy")
    after = jnp.where(at_y == lax.axis_size("gy") - 1, 0, HALO)
    ahead = jnp.where(at_y == 0, LANES, LANES - HALO)

    def final(l, start, value):
        field_out[l, start : start + 8, :] = value

    relax(
        side_tiles(fields, beside_x, sides),
        [inside, inside & ((lane < after) | (lane >= ahead))],
        heads, coef, conds, layers, False, final,
    )
    count, reaches = routed_out.shape
    line = lax.broadcasted_iota(jnp.int32, (reaches, count), 0)
    routed = lax.dot_general(
        (line == reach[...]).astype(jnp.float32),
        route[...],
        (((0,), (1,)), ((), ())),
        precision=lax.Precision.HIGHEST,
        preferred_element_type=jnp.float32,
    )
    for part in range(reaches // LANES):
        lines[part] = routed[:, part * LANES : (part + 1) * LANES]
    for part in range(reaches // LANES):
        for c in range(2):
            routed_out[c * (count // 2) : (c + 1) * (count // 2), part * LANES : (part + 1) * LANES] = (
                lines[part, pl.ds(c, count // 2, stride=2), :]
            )


def finish_flow(arrived, routed, out):
    half = arrived.shape[0]
    parts = arrived[...]
    flow = parts[:, 0:1] * routed[:half, :] + parts[:, 1:2] * routed[half:, :]
    out[...] = jnp.sum(flow + parts[:, 2:3], 0, keepdims=True)


def shifted(value, axis, by):
    count = lax.axis_size(axis)
    return lax.ppermute(value, axis, [(i, (i + by) % count) for i in range(count)])


def swapped(value, axis, first):
    count = lax.axis_size(axis)
    to = list(range(count))
    for i in range(first, count, 2):
        to[i], to[(i + 1) % count] = (i + 1) % count, i
    return lax.ppermute(value, axis, list(enumerate(to)))


def per_device(
    initial_head, conductivity, source_rate, storage_term, bed_conduct, row_cells, row_reach,
    river_section, bed_depth, route_inverse, retention, chain_heads,
):
    layers, rows, width = initial_head.shape
    fields = (initial_head, conductivity, source_rate, storage_term)
    edge = f32(4, layers, HALO, width)
    planes = -(-4 * layers // GROUPS)
    tall = rows + 2 * HALO
    side = f32(planes, tall, LANES)
    row_total = row_cells.shape[1]
    reaches = river_section.shape[1]
    cells = row_cells[0]

    def scratch(*shape):
        return pltpu.VMEM(shape, jnp.float32)

    last, first, info = call(
        front,
        (edge, edge, f32(row_total, LANES)),
        10,
        scratch=(
            pltpu.VMEM((1, row_total), jnp.int32),
            scratch(1, reaches),
            scratch(1, reaches),
            scratch(8, reaches),
            pltpu.SMEM((1,), jnp.float32),
            pltpu.SMEM((1,), jnp.int32),
            pltpu.SemaphoreType.DMA((14,)),
        ),
        anywhere=True,
        mib=60,
    )(*fields, row_reach, river_section, bed_depth, route_inverse, retention, chain_heads)
    pair_x = (shifted(last, "gx", 1), shifted(first, "gx", -1))
    info = lax.all_to_all(info, AXES, split_axis=0, concat_axis=0, tiled=True)
    for_even, for_odd = call(pack_y, (side, side), 6)(*fields, *pair_x)
    pair_y = (swapped(for_odd, "gy", 1), swapped(for_even, "gy", 0))
    pads = tall + 2 * TOP
    held = SWEEPS + 1
    sides = scratch(2, planes, tall, LANES)
    own = (
        scratch(2, 1, held, pads, LANES),
        scratch(7, 1, SWEEPS, tall, LANES),
        scratch(1, held, pads, LANES),
    )
    beds, top, strips = call(
        inner,
        (f32(row_total, LANES), f32(rows, width), f32(4, held, tall, LANES)),
        8,
        scratch=own,
        mib=16,
        micros=3,
    )(*fields, *pair_x, cells, bed_conduct)
    table = call(
        functools.partial(edges, layers), f32(rows, width), 4, scratch=(*own, sides), mib=16, micros=2
    )(strips, *pair_y, top)
    sent = call(
        leak_rows,
        f32(row_total // 2, LANES),
        4,
        scratch=(
            scratch(2, row_total // 2, LANES),
            scratch(2, row_total, LANES),
            scratch(row_total, LANES),
        ),
        micros=3,
    )(table, cells, beds, info)
    arrived = lax.all_to_all(sent, AXES, split_axis=0, concat_axis=0, tiled=True)
    head_field, routed = call(
        everywhere,
        (f32(layers, rows, width), f32(row_total, reaches)),
        10,
        scratch=(
            scratch(2, 2, layers, pads, LANES),
            scratch(7, 2, layers, tall, LANES),
            scratch(2, layers, pads, LANES),
            scratch(reaches // LANES, row_total, LANES),
            sides,
        ),
        mib=20,
        micros=5,
    )(*fields, *pair_x, *pair_y, row_reach, route_inverse[0])
    reach_flow = call(finish_flow, f32(1, reaches), 2)(arrived, routed)
    return (head_field, reach_flow)


def solution(mesh):
    placed = (
        P(None, "gx", "gy"),
        P(None, "gx", "gy"),
        P(None, "gx", "gy"),
        P(None, "gx", "gy"),
        P("gx", "gy"),
        P(AXES, None, None),
        P(AXES, None),
        P(AXES, None),
        P(AXES, None),
        P(AXES, None, None),
        P(AXES),
        P(AXES),
    )
    return jax.shard_map(
        per_device,
        mesh=mesh,
        in_specs=placed,
        out_specs=(P(None, "gx", "gy"), P(AXES, None)),
        check_vma=False,
    )
```

```python
import functools

import jax
import jax.numpy as jnp
from jax import lax
from jax.experimental import pallas as pl
from jax.experimental.pallas import tpu as pltpu
from jax.sharding import PartitionSpec as P

SWEEPS = 8
HALO = 8
LANES = 128
GROUPS = LANES // HALO
AXES = ("gx", "gy")
VMEM = pl.BlockSpec(memory_space=pltpu.VMEM)
ANY = pl.BlockSpec(memory_space=pl.ANY)
TOP, BOTTOM = HALO, 2 * HALO


def call(body, out, count, scratch=(), anywhere=False, mib=8, micros=1):
    return pl.pallas_call(
        body,
        out_shape=out,
        in_specs=[ANY if anywhere else VMEM] * count,
        out_specs=jax.tree.map(lambda _: VMEM, out),
        scratch_shapes=list(scratch),
        compiler_params=pltpu.CompilerParams(vmem_limit_bytes=mib * 1024 * 1024),
        cost_estimate=pl.CostEstimate(
            flops=0, transcendentals=0, bytes_accessed=micros * 3_000_000
        ),
    )


def f32(*shape):
    return jax.ShapeDtypeStruct(shape, jnp.float32)


def front(
    head, cond, source, storage, reach, section, depth, route, retention, heads,
    last_out, first_out, info_out,
    reach_here, section_here, depth_here, weight_here, retention_here, heads_here, sems,
):
    rows = head.shape[1]
    reaches = section.shape[1]
    edges = []
    for k, ref in enumerate((head, cond, source, storage)):
        edges.append((ref.at[:, rows - HALO :, :], last_out.at[k]))
        edges.append((ref.at[:, :HALO, :], first_out.at[k]))
    small = [
        (reach, reach_here),
        (section, section_here),
        (depth, depth_here),
        (route.at[0, reaches - 8 :, :], weight_here),
        (retention, retention_here),
        (heads, heads_here),
    ]
    copies = [pltpu.make_async_copy(a, b, sems.at[i]) for i, (a, b) in enumerate(small + edges)]
    for copy in copies:
        copy.start()
    for copy in copies[: len(small)]:
        copy.wait()
    carry = retention_here[0] * (1.0 - heads_here[0].astype(jnp.float32))
    sec = section_here[...]
    table = jnp.concatenate(
        [sec, sec - depth_here[...], weight_here[7:8, :], jnp.full((5, reaches), carry)], 0
    )
    count = reach.shape[1]
    for part in range(count // LANES):
        spots = jnp.broadcast_to(reach_here[:, part * LANES : (part + 1) * LANES], (8, LANES))
        picked = jnp.zeros((8, LANES), jnp.float32)
        for block in range(reaches // LANES):
            value = jnp.take_along_axis(
                table[:, block * LANES : (block + 1) * LANES],
                spots & (LANES - 1),
                axis=1,
                mode="promise_in_bounds",
            )
            picked = jnp.where(spots // LANES == block, value, picked)
        tall = jnp.concatenate([picked, jnp.zeros((LANES - 8, LANES), jnp.float32)], 0)
        info_out[part * LANES : (part + 1) * LANES, :] = jnp.transpose(tall)
    for copy in copies[len(small) :]:
        copy.wait()


def pack_y(head, cond, source, storage, low, high, even_out, odd_out):
    fields = (head, cond, source, storage)
    layers, rows, width = head.shape
    even_y = lax.axis_index("gy") % 2 == 0
    lane = lax.broadcasted_iota(jnp.int32, (rows + 2 * HALO, LANES), 1)
    first_sum = [None] * even_out.shape[0]
    last_sum = [None] * even_out.shape[0]
    for k in range(4):
        for l in range(layers):
            plane, group = divmod(k * layers + l, GROUPS)
            whole = tall_row(fields, (low, high), k, l)
            spread = turned(whole, group * HALO)
            if first_sum[plane] is None:
                first_sum[plane], last_sum[plane] = spread, spread
            else:
                first_sum[plane] = jnp.where(
                    lane // HALO == group, spread, first_sum[plane]
                )
                last_sum[plane] = jnp.where(
                    lane // HALO == (group - 1) % GROUPS, spread, last_sum[plane]
                )
    for plane in range(even_out.shape[0]):
        even_out[plane] = jnp.where(even_y, last_sum[plane], first_sum[plane])
        odd_out[plane] = jnp.where(even_y, first_sum[plane], last_sum[plane])


def cell_block(cells_ref, b):
    c, g = divmod(b, cells_ref.shape[0] // 16)
    cells = cells_ref[pl.ds(g * 16 + c, 8, stride=2), :]
    return cells & (LANES - 1), cells // LANES


def select(found, column, line, table):
    for r, spread in enumerate(table):
        value = jnp.take_along_axis(spread, column, axis=1, mode="promise_in_bounds")
        found = jnp.where(line == r, value, found)
    return found


def spread_rows(table):
    return [jnp.broadcast_to(table[r : r + 1, :], (8, LANES)) for r in range(table.shape[0])]


def tall_row(fields, beside_x, k, l):
    low, high = beside_x
    return jnp.concatenate([low[k, l], fields[k][l], high[k, l]], 0)


def settle(one, other, sides):
    even = lax.axis_index("gy") % 2 == 0
    for plane in range(sides.shape[1]):
        sides[0, plane] = jnp.where(even, other[plane], one[plane])
        sides[1, plane] = jnp.where(even, one[plane], other[plane])


def turned(value, by):
    return pltpu.roll(value, by % LANES, 1) if by % LANES else value


def side_tiles(fields, beside_x, sides):
    layers = fields[0].shape[0]

    def get(k, l):
        plane, group = divmod(k * layers + l, GROUPS)
        whole = tall_row(fields, beside_x, k, l)
        lane = lax.broadcasted_iota(jnp.int32, whole.shape, 1)
        both = jnp.where(lane // HALO == group, sides[1, plane], sides[0, plane])
        near = (lane < HALO) | (lane >= LANES - HALO)
        side = jnp.where(near, turned(both, -group * HALO), 0.0)
        return [whole, side]

    return get


def strip_tiles(strips, sides, layers):
    def get(k, l):
        plane, group = divmod(k * layers + l, GROUPS)
        lane = lax.broadcasted_iota(jnp.int32, sides.shape[2:], 1)
        after = turned(sides[1, plane], 2 * HALO - group * HALO)
        ahead = turned(sides[0, plane], 3 * HALO - (group - 1) % GROUPS * HALO)
        own = strips[k, l]
        inner = jnp.where(lane < 3 * HALO, after, ahead)
        return [jnp.where((lane >= 2 * HALO) & (lane < 4 * HALO), inner, own)]

    return get


def inside_rows(row):
    at_x = lax.axis_index("gx")
    first_row = jnp.where(at_x == 0, HALO, 0)
    last_row = jnp.where(at_x == lax.axis_size("gx") - 1, row.shape[0] - HALO, row.shape[0])
    return (row >= first_row) & (row < last_row)


def beside(tiles):
    lane = lax.broadcasted_iota(jnp.int32, tiles[0].shape, 1)
    ahead = [pltpu.roll(one, LANES - 1, 1) for one in tiles]
    behind = [pltpu.roll(one, 1, 1) for one in tiles]
    if len(tiles) == 1:
        return ahead, behind
    east = [jnp.where(lane == LANES - 1, ahead[1 - t], ahead[t]) for t in range(2)]
    west = [jnp.where(lane == 0, behind[1 - t], behind[t]) for t in range(2)]
    return east, west


def set_coefs(get, conds, coef, l, bottom):
    tiles, rows = conds.shape[0], conds.shape[2]
    span = slice(TOP, rows - TOP)
    east, west = beside([conds[t, l, span, :] for t in range(tiles)])
    storage, source = get(3, l), get(2, l)
    for t in range(tiles):
        mid = conds[t, l, span, :]
        inside = mid > 0.0

        def face(near):
            return jnp.where(inside & (near > 0.0), 0.5 * (mid + near), 0.0)

        faces = [
            face(east[t]),
            face(west[t]),
            face(conds[t, l, TOP + 1 : rows - TOP + 1, :]),
            face(conds[t, l, TOP - 1 : rows - TOP - 1, :]),
            0.5 * (mid + conds[t, l - 1, span, :]) if l else None,
            None if bottom else 0.5 * (mid + conds[t, l + 1, span, :]),
        ]
        total = storage[t]
        for one in faces:
            if one is not None:
                total = total + one
        inverse = jnp.where(inside, 1.0 / jnp.where(inside, total, 1.0), 0.0)
        for k, one in enumerate(faces):
            if one is not None:
                coef[k, t, l] = one * inverse
        coef[6, t, l] = source[t] * inverse


def relax(get, masks, heads, coef, conds, layers, cone, final):
    tiles, held, rows = heads.shape[1:4]
    edge = jnp.zeros((TOP, LANES), jnp.float32)
    for l in range(held):
        for t, value in enumerate(get(0, l)):
            heads[0, t, l, TOP : rows - TOP, :] = value
        for t, value in enumerate(get(1, l)):
            conds[t, l, TOP : rows - TOP, :] = jnp.where(masks[t], value, 0.0)
            for span in (slice(0, TOP), slice(rows - TOP, rows)):
                conds[t, l, span, :] = edge
                heads[0, t, l, span, :] = edge
                heads[1, t, l, span, :] = edge
    for l in range(held - 1 if cone else held):
        set_coefs(get, conds, coef, l, l + 1 == layers)
    for time in range(SWEEPS):
        last_sweep = time == SWEEPS - 1
        margin = BOTTOM if last_sweep else TOP
        many = SWEEPS - time if cone else layers
        old = time % 2
        for start in range(margin, rows - margin, 8):
            span = slice(start, start + 8)
            mids = [
                [heads[old, t, l, span, :] for t in range(tiles)]
                for l in range(min(many + 1, layers))
            ]
            for l in range(many):
                east, west = beside(mids[l])
                at = slice(start - TOP, start - TOP + 8)
                for t in range(1 if last_sweep else tiles):
                    out = coef[6, t, l, at, :] + coef[0, t, l, at, :] * east[t]
                    out = out + coef[1, t, l, at, :] * west[t]
                    out = out + coef[2, t, l, at, :] * heads[old, t, l, start + 1 : start + 9, :]
                    out = out + coef[3, t, l, at, :] * heads[old, t, l, start - 1 : start + 7, :]
                    if l:
                        out = out + coef[4, t, l, at, :] * mids[l - 1][t]
                    if l + 1 < layers:
                        out = out + coef[5, t, l, at, :] * mids[l + 1][t]
                    if last_sweep:
                        final(l, start - BOTTOM, out)
                    else:
                        heads[1 - old, t, l, span, :] = out


def inner(
    head, cond, source, storage, low, high, cells, bed,
    beds_out, found_out, strips_out, heads, coef, conds, top,
):
    fields = (head, cond, source, storage)
    beside_x = (low, high)
    layers, rows, width = head.shape
    tall = rows + 2 * HALO
    lane = lax.broadcasted_iota(jnp.int32, (tall, LANES), 1)
    for k in range(4):
        for l in range(SWEEPS + 1 if k < 2 else SWEEPS):
            whole = tall_row(fields, beside_x, k, l)
            strip = jnp.where(lane < 2 * HALO, turned(whole, 2 * HALO), turned(whole, 4 * HALO))
            strips_out[k, l] = jnp.where(lane < 6 * HALO, strip, 0.0)

    def final(l, start, value):
        top[start : start + 8, :] = value

    inside = inside_rows(lax.broadcasted_iota(jnp.int32, (tall, LANES), 0))
    relax(
        lambda k, l: [tall_row(fields, beside_x, k, l)], [inside],
        heads, coef, conds, layers, True, final,
    )
    bed_table, head_table = spread_rows(bed[...]), spread_rows(top[...])
    for b in range(cells.shape[0] // 8):
        column, line = cell_block(cells, b)
        span = slice(b * 8, (b + 1) * 8)
        nothing = jnp.zeros((8, LANES), jnp.float32)
        beds_out[span, :] = select(nothing, column, line, bed_table)
        found_out[span, :] = select(nothing, column, line, head_table)


def edges(layers, strips, other_y, one_y, ends_out, heads, coef, conds, sides):
    settle(one_y, other_y, sides)
    tall = strips.shape[2]
    lane = lax.broadcasted_iota(jnp.int32, (tall, LANES), 1)
    at_y = lax.axis_index("gy")
    first = (at_y == 0) & (lane >= 3 * HALO) & (lane < 4 * HALO)
    last = (at_y == lax.axis_size("gy") - 1) & (lane >= 2 * HALO) & (lane < 3 * HALO)
    inside = inside_rows(lax.broadcasted_iota(jnp.int32, (tall, LANES), 0))
    mask = inside & ~first & ~last & (lane < 6 * HALO)

    def final(l, start, value):
        column = lax.broadcasted_iota(jnp.int32, value.shape, 1)
        row = lax.broadcasted_iota(jnp.int32, value.shape, 0)
        ends = jnp.where(column < HALO, turned(value, -4 * HALO), value)
        ends = jnp.where(column < 2 * HALO, ends, 0.0)
        line = jnp.zeros_like(value)
        for r in range(8):
            line = line + jnp.where(row == r, turned(ends, r * 2 * HALO), 0.0)
        ends_out[start // 8 : start // 8 + 1, :] = jnp.sum(line, 0, keepdims=True)

    relax(
        strip_tiles(strips, sides, layers), [mask],
        heads, coef, conds, layers, True, final,
    )


def leak_rows(found, ends, cells, beds, info, send_out, weights, levels, leaks):
    peers = info.shape[0] // 2
    groups = peers // 8
    for c in range(2):
        for g in range(groups):
            detail = info[pl.ds(g * 16 + c, 8, stride=2), :]
            span = slice((c * groups + g) * 8, (c * groups + g + 1) * 8)
            for k in range(2):
                levels[k, span, :] = jnp.broadcast_to(detail[:, k : k + 1], (8, LANES))

    def running(value, lane, length):
        step = 1
        while step < length:
            value = value * jnp.where(lane % length >= step, pltpu.roll(value, step, 1), 1.0)
            step *= 2
        return value

    sub = lax.broadcasted_iota(jnp.int32, (peers, LANES), 0)
    lane = lax.broadcasted_iota(jnp.int32, (peers, LANES), 1)
    details = [info[pl.ds(c, peers, stride=2), :] for c in range(2)]
    carry_row = jnp.sum(jnp.where(sub == lane, details[0][:, 3:4], 0.0), 0, keepdims=True)
    sub, lane = sub[:8], lane[:8]
    within = running(jnp.where(lane % 8 > sub, carry_row, 1.0), lane, 8)
    own = jnp.where(lane % 8 > sub, within, 0.0)
    block = lax.broadcasted_iota(jnp.int32, (groups, LANES), 0)
    wide = lax.broadcasted_iota(jnp.int32, (groups, LANES), 1)
    beyond = running(jnp.where(wide > block * 8 + 7, carry_row, 1.0), wide, LANES)
    for g in range(groups):
        through = within[:, g * 8 + 7 : g * 8 + 8] * beyond[g : g + 1, :]
        product = jnp.where(lane // 8 == g, own, jnp.where(lane // 8 > g, through, 0.0))
        for c in range(2):
            weights[c, g * 8 : (g + 1) * 8, :] = product * details[c][g * 8 : (g + 1) * 8, 2:3]

    table = spread_rows(ends[...])
    for b in range(2 * groups):
        column, line = cell_block(cells, b)
        span = slice(b * 8, (b + 1) * 8)
        near = (column < HALO) | (column >= LANES - HALO)
        at = line * (2 * HALO) + jnp.where(column < HALO, column, column - (LANES - 2 * HALO))
        value = select(
            found[span, :], at & (LANES - 1), jnp.where(near, at // LANES, -1), table
        )
        leaks[span, :] = beds[span, :] * (
            jnp.maximum(value, levels[1, span, :]) - levels[0, span, :]
        )
    eight = lax.broadcasted_iota(jnp.int32, (8, LANES), 1)
    flow = jnp.zeros((8, LANES), jnp.float32)
    sums = []
    for g in range(groups):
        span = slice(g * 8, (g + 1) * 8)
        row_leak = [
            jnp.sum(leaks[c * peers + g * 8 : c * peers + (g + 1) * 8, :], 1, keepdims=True)
            for c in range(2)
        ]
        for c in range(2):
            flow = flow + weights[c, span, :] * row_leak[c]
        sums.append(jnp.where(eight == 0, row_leak[0], row_leak[1]))
    flow = jnp.sum(flow, 0, keepdims=True)
    for g in range(groups):
        mine = lax.broadcasted_iota(jnp.int32, (8, LANES), 0) + g * 8 == eight
        column = jnp.sum(jnp.where(mine, flow, 0.0), 1, keepdims=True)
        send_out[g * 8 : (g + 1) * 8, :] = jnp.where(eight == 2, column, sums[g])


def everywhere(
    head, cond, source, storage, low, high, other_y, one_y, reach, route,
    field_out, routed_out, heads, coef, conds, lines, sides,
):
    fields = (head, cond, source, storage)
    beside_x = (low, high)
    settle(one_y, other_y, sides)
    layers, rows, width = head.shape
    tall = rows + 2 * HALO
    lane = lax.broadcasted_iota(jnp.int32, (tall, LANES), 1)
    inside = inside_rows(lax.broadcasted_iota(jnp.int32, (tall, LANES), 0))
    at_y = lax.axis_index("gy")
    after = jnp.where(at_y == lax.axis_size("gy") - 1, 0, HALO)
    ahead = jnp.where(at_y == 0, LANES, LANES - HALO)

    def final(l, start, value):
        field_out[l, start : start + 8, :] = value

    relax(
        side_tiles(fields, beside_x, sides),
        [inside, inside & ((lane < after) | (lane >= ahead))],
        heads, coef, conds, layers, False, final,
    )
    count, reaches = routed_out.shape
    line = lax.broadcasted_iota(jnp.int32, (reaches, count), 0)
    routed = lax.dot_general(
        (line == reach[...]).astype(jnp.float32),
        route[...],
        (((0,), (1,)), ((), ())),
        precision=lax.Precision.HIGHEST,
        preferred_element_type=jnp.float32,
    )
    for part in range(reaches // LANES):
        lines[part] = routed[:, part * LANES : (part + 1) * LANES]
    for part in range(reaches // LANES):
        for c in range(2):
            routed_out[c * (count // 2) : (c + 1) * (count // 2), part * LANES : (part + 1) * LANES] = (
                lines[part, pl.ds(c, count // 2, stride=2), :]
            )


def finish_flow(arrived, routed, out):
    half = arrived.shape[0]
    parts = arrived[...]
    flow = parts[:, 0:1] * routed[:half, :] + parts[:, 1:2] * routed[half:, :]
    out[...] = jnp.sum(flow + parts[:, 2:3], 0, keepdims=True)


def shifted(value, axis, by):
    count = lax.axis_size(axis)
    return lax.ppermute(value, axis, [(i, (i + by) % count) for i in range(count)])


def swapped(value, axis, first):
    count = lax.axis_size(axis)
    to = list(range(count))
    for i in range(first, count, 2):
        to[i], to[(i + 1) % count] = (i + 1) % count, i
    return lax.ppermute(value, axis, list(enumerate(to)))


def per_device(
    initial_head, conductivity, source_rate, storage_term, bed_conduct, row_cells, row_reach,
    river_section, bed_depth, route_inverse, retention, chain_heads,
):
    layers, rows, width = initial_head.shape
    fields = (initial_head, conductivity, source_rate, storage_term)
    edge = f32(4, layers, HALO, width)
    planes = -(-4 * layers // GROUPS)
    tall = rows + 2 * HALO
    side = f32(planes, tall, LANES)
    row_total = row_cells.shape[1]
    reaches = river_section.shape[1]
    cells = row_cells[0]

    def scratch(*shape):
        return pltpu.VMEM(shape, jnp.float32)

    last, first, info = call(
        front,
        (edge, edge, f32(row_total, LANES)),
        10,
        scratch=(
            pltpu.VMEM((1, row_total), jnp.int32),
            scratch(1, reaches),
            scratch(1, reaches),
            scratch(8, reaches),
            pltpu.SMEM((1,), jnp.float32),
            pltpu.SMEM((1,), jnp.int32),
            pltpu.SemaphoreType.DMA((14,)),
        ),
        anywhere=True,
        mib=60,
    )(*fields, row_reach, river_section, bed_depth, route_inverse, retention, chain_heads)
    pair_x = (shifted(last, "gx", 1), shifted(first, "gx", -1))
    info = lax.all_to_all(info, AXES, split_axis=0, concat_axis=0, tiled=True)
    for_even, for_odd = call(pack_y, (side, side), 6)(*fields, *pair_x)
    pair_y = (swapped(for_odd, "gy", 1), swapped(for_even, "gy", 0))
    pads = tall + 2 * TOP
    held = SWEEPS + 1
    sides = scratch(2, planes, tall, LANES)
    own = (
        scratch(2, 1, held, pads, LANES),
        scratch(7, 1, SWEEPS, tall, LANES),
        scratch(1, held, pads, LANES),
    )
    beds, found, strips = call(
        inner,
        (f32(row_total, LANES), f32(row_total, LANES), f32(4, held, tall, LANES)),
        8,
        scratch=(*own, scratch(rows, LANES)),
        mib=16,
        micros=3,
    )(*fields, *pair_x, cells, bed_conduct)
    ends = call(
        functools.partial(edges, layers),
        f32(rows // 8, LANES),
        3,
        scratch=(*own, sides),
        mib=16,
        micros=2,
    )(strips, *pair_y)
    sent = call(
        leak_rows,
        f32(row_total // 2, LANES),
        5,
        scratch=(
            scratch(2, row_total // 2, LANES),
            scratch(2, row_total, LANES),
            scratch(row_total, LANES),
        ),
        micros=3,
    )(found, ends, cells, beds, info)
    arrived = lax.all_to_all(sent, AXES, split_axis=0, concat_axis=0, tiled=True)
    head_field, routed = call(
        everywhere,
        (f32(layers, rows, width), f32(row_total, reaches)),
        10,
        scratch=(
            scratch(2, 2, layers, pads, LANES),
            scratch(7, 2, layers, tall, LANES),
            scratch(2, layers, pads, LANES),
            scratch(reaches // LANES, row_total, LANES),
            sides,
        ),
        mib=20,
        micros=5,
    )(*fields, *pair_x, *pair_y, row_reach, route_inverse[0])
    reach_flow = call(finish_flow, f32(1, reaches), 2)(arrived, routed)
    return (head_field, reach_flow)


def solution(mesh):
    placed = (
        P(None, "gx", "gy"),
        P(None, "gx", "gy"),
        P(None, "gx", "gy"),
        P(None, "gx", "gy"),
        P("gx", "gy"),
        P(AXES, None, None),
        P(AXES, None),
        P(AXES, None),
        P(AXES, None),
        P(AXES, None, None),
        P(AXES),
        P(AXES),
    )
    return jax.shard_map(
        per_device,
        mesh=mesh,
        in_specs=placed,
        out_specs=(P(None, "gx", "gy"), P(AXES, None)),
        check_vma=False,
    )
```

```python
import functools

import jax
import jax.numpy as jnp
from jax import lax
from jax.experimental import pallas as pl
from jax.experimental.pallas import tpu as pltpu
from jax.sharding import PartitionSpec as P

SWEEPS = 8
HALO = 8
LANES = 128
GROUPS = LANES // HALO
AXES = ("gx", "gy")
VMEM = pl.BlockSpec(memory_space=pltpu.VMEM)
ANY = pl.BlockSpec(memory_space=pl.ANY)
TOP, BOTTOM = HALO, 2 * HALO


def call(body, out, count, scratch=(), anywhere=False, mib=8, micros=1):
    return pl.pallas_call(
        body,
        out_shape=out,
        in_specs=[ANY if anywhere else VMEM] * count,
        out_specs=jax.tree.map(lambda _: VMEM, out),
        scratch_shapes=list(scratch),
        compiler_params=pltpu.CompilerParams(vmem_limit_bytes=mib * 1024 * 1024),
        cost_estimate=pl.CostEstimate(
            flops=0, transcendentals=0, bytes_accessed=micros * 3_000_000
        ),
    )


def f32(*shape):
    return jax.ShapeDtypeStruct(shape, jnp.float32)


def front(
    head, cond, source, storage, reach, section, depth, route, retention, heads,
    last_out, first_out, info_out,
    reach_here, section_here, depth_here, weight_here, retention_here, heads_here, sems,
):
    rows = head.shape[1]
    reaches = section.shape[1]
    edges = []
    for k, ref in enumerate((head, cond, source, storage)):
        edges.append((ref.at[:, rows - HALO :, :], last_out.at[k]))
        edges.append((ref.at[:, :HALO, :], first_out.at[k]))
    small = [
        (reach, reach_here),
        (section, section_here),
        (depth, depth_here),
        (route.at[0, reaches - 8 :, :], weight_here),
        (retention, retention_here),
        (heads, heads_here),
    ]
    copies = [pltpu.make_async_copy(a, b, sems.at[i]) for i, (a, b) in enumerate(small + edges)]
    for copy in copies:
        copy.start()
    for copy in copies[: len(small)]:
        copy.wait()
    carry = retention_here[0] * (1.0 - heads_here[0].astype(jnp.float32))
    sec = section_here[...]
    table = jnp.concatenate(
        [sec, sec - depth_here[...], weight_here[7:8, :], jnp.full((5, reaches), carry)], 0
    )
    count = reach.shape[1]
    for part in range(count // LANES):
        spots = jnp.broadcast_to(reach_here[:, part * LANES : (part + 1) * LANES], (8, LANES))
        picked = jnp.zeros((8, LANES), jnp.float32)
        for block in range(reaches // LANES):
            value = jnp.take_along_axis(
                table[:, block * LANES : (block + 1) * LANES],
                spots & (LANES - 1),
                axis=1,
                mode="promise_in_bounds",
            )
            picked = jnp.where(spots // LANES == block, value, picked)
        tall = jnp.concatenate([picked, jnp.zeros((LANES - 8, LANES), jnp.float32)], 0)
        info_out[part * LANES : (part + 1) * LANES, :] = jnp.transpose(tall)
    for copy in copies[len(small) :]:
        copy.wait()


def pack_y(head, cond, source, storage, low, high, even_out, odd_out):
    fields = (head, cond, source, storage)
    layers, rows, width = head.shape
    even_y = lax.axis_index("gy") % 2 == 0
    lane = lax.broadcasted_iota(jnp.int32, (rows + 2 * HALO, LANES), 1)
    first_sum = [None] * even_out.shape[0]
    last_sum = [None] * even_out.shape[0]
    for k in range(4):
        for l in range(layers):
            plane, group = divmod(k * layers + l, GROUPS)
            whole = tall_row(fields, (low, high), k, l)
            spread = turned(whole, group * HALO)
            if first_sum[plane] is None:
                first_sum[plane], last_sum[plane] = spread, spread
            else:
                first_sum[plane] = jnp.where(
                    lane // HALO == group, spread, first_sum[plane]
                )
                last_sum[plane] = jnp.where(
                    lane // HALO == (group - 1) % GROUPS, spread, last_sum[plane]
                )
    for plane in range(even_out.shape[0]):
        even_out[plane] = jnp.where(even_y, last_sum[plane], first_sum[plane])
        odd_out[plane] = jnp.where(even_y, first_sum[plane], last_sum[plane])


def cell_block(cells_ref, b):
    c, g = divmod(b, cells_ref.shape[0] // 16)
    cells = cells_ref[pl.ds(g * 16 + c, 8, stride=2), :]
    return cells & (LANES - 1), cells // LANES


def select(found, column, line, table):
    for r, spread in enumerate(table):
        value = jnp.take_along_axis(spread, column, axis=1, mode="promise_in_bounds")
        found = jnp.where(line == r, value, found)
    return found


def spread_rows(table):
    return [jnp.broadcast_to(table[r : r + 1, :], (8, LANES)) for r in range(table.shape[0])]


def tall_row(fields, beside_x, k, l):
    low, high = beside_x
    return jnp.concatenate([low[k, l], fields[k][l], high[k, l]], 0)


def settle(one, other, sides):
    even = lax.axis_index("gy") % 2 == 0
    for plane in range(sides.shape[1]):
        sides[0, plane] = jnp.where(even, other[plane], one[plane])
        sides[1, plane] = jnp.where(even, one[plane], other[plane])


def turned(value, by):
    return pltpu.roll(value, by % LANES, 1) if by % LANES else value


def side_tiles(fields, beside_x, sides):
    layers = fields[0].shape[0]

    def get(k, l):
        plane, group = divmod(k * layers + l, GROUPS)
        whole = tall_row(fields, beside_x, k, l)
        lane = lax.broadcasted_iota(jnp.int32, whole.shape, 1)
        both = jnp.where(lane // HALO == group, sides[1, plane], sides[0, plane])
        near = (lane < HALO) | (lane >= LANES - HALO)
        side = jnp.where(near, turned(both, -group * HALO), 0.0)
        return [whole, side]

    return get


def strip_tiles(strips, sides, layers):
    def get(k, l):
        plane, group = divmod(k * layers + l, GROUPS)
        lane = lax.broadcasted_iota(jnp.int32, sides.shape[2:], 1)
        after = turned(sides[1, plane], 2 * HALO - group * HALO)
        ahead = turned(sides[0, plane], 3 * HALO - (group - 1) % GROUPS * HALO)
        own = strips[k, l]
        inner = jnp.where(lane < 3 * HALO, after, ahead)
        return [jnp.where((lane >= 2 * HALO) & (lane < 4 * HALO), inner, own)]

    return get


def inside_rows(row):
    at_x = lax.axis_index("gx")
    first_row = jnp.where(at_x == 0, HALO, 0)
    last_row = jnp.where(at_x == lax.axis_size("gx") - 1, row.shape[0] - HALO, row.shape[0])
    return (row >= first_row) & (row < last_row)


def beside(tiles):
    lane = lax.broadcasted_iota(jnp.int32, tiles[0].shape, 1)
    ahead = [pltpu.roll(one, LANES - 1, 1) for one in tiles]
    behind = [pltpu.roll(one, 1, 1) for one in tiles]
    if len(tiles) == 1:
        return ahead, behind
    east = [jnp.where(lane == LANES - 1, ahead[1 - t], ahead[t]) for t in range(2)]
    west = [jnp.where(lane == 0, behind[1 - t], behind[t]) for t in range(2)]
    return east, west


def set_coefs(get, conds, coef, l, bottom):
    tiles, rows = conds.shape[0], conds.shape[2]
    span = slice(TOP, rows - TOP)
    east, west = beside([conds[t, l, span, :] for t in range(tiles)])
    storage, source = get(3, l), get(2, l)
    for t in range(tiles):
        mid = conds[t, l, span, :]
        inside = mid > 0.0

        def face(near):
            return jnp.where(inside & (near > 0.0), 0.5 * (mid + near), 0.0)

        faces = [
            face(east[t]),
            face(west[t]),
            face(conds[t, l, TOP + 1 : rows - TOP + 1, :]),
            face(conds[t, l, TOP - 1 : rows - TOP - 1, :]),
            0.5 * (mid + conds[t, l - 1, span, :]) if l else None,
            None if bottom else 0.5 * (mid + conds[t, l + 1, span, :]),
        ]
        total = storage[t]
        for one in faces:
            if one is not None:
                total = total + one
        inverse = jnp.where(inside, 1.0 / jnp.where(inside, total, 1.0), 0.0)
        for k, one in enumerate(faces):
            if one is not None:
                coef[k, t, l] = one * inverse
        coef[6, t, l] = source[t] * inverse


def relax(get, masks, heads, coef, conds, layers, cone, final):
    tiles, held, rows = heads.shape[1:4]
    edge = jnp.zeros((TOP, LANES), jnp.float32)
    for l in range(held):
        for t, value in enumerate(get(0, l)):
            heads[0, t, l, TOP : rows - TOP, :] = value
        for t, value in enumerate(get(1, l)):
            conds[t, l, TOP : rows - TOP, :] = jnp.where(masks[t], value, 0.0)
            for span in (slice(0, TOP), slice(rows - TOP, rows)):
                conds[t, l, span, :] = edge
                heads[0, t, l, span, :] = edge
                heads[1, t, l, span, :] = edge
    for l in range(held - 1 if cone else held):
        set_coefs(get, conds, coef, l, l + 1 == layers)
    for time in range(SWEEPS):
        last_sweep = time == SWEEPS - 1
        margin = BOTTOM if last_sweep else TOP
        many = SWEEPS - time if cone else layers
        old = time % 2
        for start in range(margin, rows - margin, 8):
            span = slice(start, start + 8)
            mids = [
                [heads[old, t, l, span, :] for t in range(tiles)]
                for l in range(min(many + 1, layers))
            ]
            main_rows = BOTTOM <= start < rows - BOTTOM
            for l in range(many if main_rows or not cone else many - 1):
                east, west = beside(mids[l])
                at = slice(start - TOP, start - TOP + 8)
                for t in range(1 if last_sweep else tiles):
                    out = coef[6, t, l, at, :] + coef[0, t, l, at, :] * east[t]
                    out = out + coef[1, t, l, at, :] * west[t]
                    out = out + coef[2, t, l, at, :] * heads[old, t, l, start + 1 : start + 9, :]
                    out = out + coef[3, t, l, at, :] * heads[old, t, l, start - 1 : start + 7, :]
                    if l:
                        out = out + coef[4, t, l, at, :] * mids[l - 1][t]
                    if l + 1 < layers:
                        out = out + coef[5, t, l, at, :] * mids[l + 1][t]
                    if last_sweep:
                        final(l, start - BOTTOM, out)
                    else:
                        heads[1 - old, t, l, span, :] = out


def inner(
    head, cond, source, storage, low, high, cells, bed,
    beds_out, found_out, strips_out, heads, coef, conds, top,
):
    fields = (head, cond, source, storage)
    beside_x = (low, high)
    layers, rows, width = head.shape
    tall = rows + 2 * HALO
    lane = lax.broadcasted_iota(jnp.int32, (tall, LANES), 1)
    for k in range(4):
        for l in range(SWEEPS + 1 if k < 2 else SWEEPS):
            whole = tall_row(fields, beside_x, k, l)
            strip = jnp.where(lane < 2 * HALO, turned(whole, 2 * HALO), turned(whole, 4 * HALO))
            strips_out[k, l] = jnp.where(lane < 6 * HALO, strip, 0.0)

    def final(l, start, value):
        top[start : start + 8, :] = value

    inside = inside_rows(lax.broadcasted_iota(jnp.int32, (tall, LANES), 0))
    relax(
        lambda k, l: [tall_row(fields, beside_x, k, l)], [inside],
        heads, coef, conds, layers, True, final,
    )
    bed_table, head_table = spread_rows(bed[...]), spread_rows(top[...])
    for b in range(cells.shape[0] // 8):
        column, line = cell_block(cells, b)
        span = slice(b * 8, (b + 1) * 8)
        picked = [jnp.zeros((8, LANES), jnp.float32)] * 2
        for r in range(rows):
            mine = line == r
            for k, spread in enumerate((bed_table[r], head_table[r])):
                value = jnp.take_along_axis(spread, column, axis=1, mode="promise_in_bounds")
                picked[k] = jnp.where(mine, value, picked[k])
        beds_out[span, :], found_out[span, :] = picked


def edges(layers, strips, other_y, one_y, ends_out, heads, coef, conds, sides):
    settle(one_y, other_y, sides)
    tall = strips.shape[2]
    lane = lax.broadcasted_iota(jnp.int32, (tall, LANES), 1)
    at_y = lax.axis_index("gy")
    first = (at_y == 0) & (lane >= 3 * HALO) & (lane < 4 * HALO)
    last = (at_y == lax.axis_size("gy") - 1) & (lane >= 2 * HALO) & (lane < 3 * HALO)
    inside = inside_rows(lax.broadcasted_iota(jnp.int32, (tall, LANES), 0))
    mask = inside & ~first & ~last & (lane < 6 * HALO)

    def final(l, start, value):
        column = lax.broadcasted_iota(jnp.int32, value.shape, 1)
        row = lax.broadcasted_iota(jnp.int32, value.shape, 0)
        ends = jnp.where(column < HALO, turned(value, -4 * HALO), value)
        ends = jnp.where(column < 2 * HALO, ends, 0.0)
        line = jnp.zeros_like(value)
        for r in range(8):
            line = line + jnp.where(row == r, turned(ends, r * 2 * HALO), 0.0)
        ends_out[start // 8 : start // 8 + 1, :] = jnp.sum(line, 0, keepdims=True)

    relax(
        strip_tiles(strips, sides, layers), [mask],
        heads, coef, conds, layers, True, final,
    )


def leak_rows(found, ends, cells, beds, info, send_out, weights, levels, leaks):
    peers = info.shape[0] // 2
    groups = peers // 8
    for c in range(2):
        for g in range(groups):
            detail = info[pl.ds(g * 16 + c, 8, stride=2), :]
            span = slice((c * groups + g) * 8, (c * groups + g + 1) * 8)
            for k in range(2):
                levels[k, span, :] = jnp.broadcast_to(detail[:, k : k + 1], (8, LANES))

    def running(value, lane, length):
        step = 1
        while step < length:
            value = value * jnp.where(lane % length >= step, pltpu.roll(value, step, 1), 1.0)
            step *= 2
        return value

    sub = lax.broadcasted_iota(jnp.int32, (peers, LANES), 0)
    lane = lax.broadcasted_iota(jnp.int32, (peers, LANES), 1)
    details = [info[pl.ds(c, peers, stride=2), :] for c in range(2)]
    carry_row = jnp.sum(jnp.where(sub == lane, details[0][:, 3:4], 0.0), 0, keepdims=True)
    sub, lane = sub[:8], lane[:8]
    within = running(jnp.where(lane % 8 > sub, carry_row, 1.0), lane, 8)
    own = jnp.where(lane % 8 > sub, within, 0.0)
    block = lax.broadcasted_iota(jnp.int32, (groups, LANES), 0)
    wide = lax.broadcasted_iota(jnp.int32, (groups, LANES), 1)
    beyond = running(jnp.where(wide > block * 8 + 7, carry_row, 1.0), wide, LANES)
    for g in range(groups):
        through = within[:, g * 8 + 7 : g * 8 + 8] * beyond[g : g + 1, :]
        product = jnp.where(lane // 8 == g, own, jnp.where(lane // 8 > g, through, 0.0))
        for c in range(2):
            weights[c, g * 8 : (g + 1) * 8, :] = product * details[c][g * 8 : (g + 1) * 8, 2:3]

    table = spread_rows(ends[...])
    for b in range(2 * groups):
        column, line = cell_block(cells, b)
        span = slice(b * 8, (b + 1) * 8)
        near = (column < HALO) | (column >= LANES - HALO)
        at = line * (2 * HALO) + jnp.where(column < HALO, column, column - (LANES - 2 * HALO))
        value = select(
            found[span, :], at & (LANES - 1), jnp.where(near, at // LANES, -1), table
        )
        leaks[span, :] = beds[span, :] * (
            jnp.maximum(value, levels[1, span, :]) - levels[0, span, :]
        )
    eight = lax.broadcasted_iota(jnp.int32, (8, LANES), 1)
    flow = jnp.zeros((8, LANES), jnp.float32)
    sums = []
    for g in range(groups):
        span = slice(g * 8, (g + 1) * 8)
        row_leak = [
            jnp.sum(leaks[c * peers + g * 8 : c * peers + (g + 1) * 8, :], 1, keepdims=True)
            for c in range(2)
        ]
        for c in range(2):
            flow = flow + weights[c, span, :] * row_leak[c]
        sums.append(jnp.where(eight == 0, row_leak[0], row_leak[1]))
    flow = jnp.sum(flow, 0, keepdims=True)
    for g in range(groups):
        mine = lax.broadcasted_iota(jnp.int32, (8, LANES), 0) + g * 8 == eight
        column = jnp.sum(jnp.where(mine, flow, 0.0), 1, keepdims=True)
        send_out[g * 8 : (g + 1) * 8, :] = jnp.where(eight == 2, column, sums[g])


def everywhere(
    head, cond, source, storage, low, high, other_y, one_y, reach, route,
    field_out, routed_out, heads, coef, conds, lines, sides,
):
    fields = (head, cond, source, storage)
    beside_x = (low, high)
    settle(one_y, other_y, sides)
    layers, rows, width = head.shape
    tall = rows + 2 * HALO
    lane = lax.broadcasted_iota(jnp.int32, (tall, LANES), 1)
    inside = inside_rows(lax.broadcasted_iota(jnp.int32, (tall, LANES), 0))
    at_y = lax.axis_index("gy")
    after = jnp.where(at_y == lax.axis_size("gy") - 1, 0, HALO)
    ahead = jnp.where(at_y == 0, LANES, LANES - HALO)

    def final(l, start, value):
        field_out[l, start : start + 8, :] = value

    relax(
        side_tiles(fields, beside_x, sides),
        [inside, inside & ((lane < after) | (lane >= ahead))],
        heads, coef, conds, layers, False, final,
    )
    count, reaches = routed_out.shape
    line = lax.broadcasted_iota(jnp.int32, (reaches, count), 0)
    routed = lax.dot_general(
        (line == reach[...]).astype(jnp.float32),
        route[...],
        (((0,), (1,)), ((), ())),
        precision=lax.Precision.HIGHEST,
        preferred_element_type=jnp.float32,
    )
    for part in range(reaches // LANES):
        lines[part] = routed[:, part * LANES : (part + 1) * LANES]
    for part in range(reaches // LANES):
        for c in range(2):
            routed_out[c * (count // 2) : (c + 1) * (count // 2), part * LANES : (part + 1) * LANES] = (
                lines[part, pl.ds(c, count // 2, stride=2), :]
            )


def finish_flow(arrived, routed, out):
    half = arrived.shape[0]
    parts = arrived[...]
    flow = parts[:, 0:1] * routed[:half, :] + parts[:, 1:2] * routed[half:, :]
    out[...] = jnp.sum(flow + parts[:, 2:3], 0, keepdims=True)


def shifted(value, axis, by):
    count = lax.axis_size(axis)
    return lax.ppermute(value, axis, [(i, (i + by) % count) for i in range(count)])


def swapped(value, axis, first):
    count = lax.axis_size(axis)
    to = list(range(count))
    for i in range(first, count, 2):
        to[i], to[(i + 1) % count] = (i + 1) % count, i
    return lax.ppermute(value, axis, list(enumerate(to)))


def per_device(
    initial_head, conductivity, source_rate, storage_term, bed_conduct, row_cells, row_reach,
    river_section, bed_depth, route_inverse, retention, chain_heads,
):
    layers, rows, width = initial_head.shape
    fields = (initial_head, conductivity, source_rate, storage_term)
    edge = f32(4, layers, HALO, width)
    planes = -(-4 * layers // GROUPS)
    tall = rows + 2 * HALO
    side = f32(planes, tall, LANES)
    row_total = row_cells.shape[1]
    reaches = river_section.shape[1]
    cells = row_cells[0]

    def scratch(*shape):
        return pltpu.VMEM(shape, jnp.float32)

    last, first, info = call(
        front,
        (edge, edge, f32(row_total, LANES)),
        10,
        scratch=(
            pltpu.VMEM((1, row_total), jnp.int32),
            scratch(1, reaches),
            scratch(1, reaches),
            scratch(8, reaches),
            pltpu.SMEM((1,), jnp.float32),
            pltpu.SMEM((1,), jnp.int32),
            pltpu.SemaphoreType.DMA((14,)),
        ),
        anywhere=True,
        mib=60,
    )(*fields, row_reach, river_section, bed_depth, route_inverse, retention, chain_heads)
    pair_x = (shifted(last, "gx", 1), shifted(first, "gx", -1))
    info = lax.all_to_all(info, AXES, split_axis=0, concat_axis=0, tiled=True)
    for_even, for_odd = call(pack_y, (side, side), 6)(*fields, *pair_x)
    pair_y = (swapped(for_odd, "gy", 1), swapped(for_even, "gy", 0))
    pads = tall + 2 * TOP
    held = SWEEPS + 1
    sides = scratch(2, planes, tall, LANES)
    own = (
        scratch(2, 1, held, pads, LANES),
        scratch(7, 1, SWEEPS, tall, LANES),
        scratch(1, held, pads, LANES),
    )
    beds, found, strips = call(
        inner,
        (f32(row_total, LANES), f32(row_total, LANES), f32(4, held, tall, LANES)),
        8,
        scratch=(*own, scratch(rows, LANES)),
        mib=16,
        micros=3,
    )(*fields, *pair_x, cells, bed_conduct)
    ends = call(
        functools.partial(edges, layers),
        f32(rows // 8, LANES),
        3,
        scratch=(*own, sides),
        mib=16,
        micros=2,
    )(strips, *pair_y)
    sent = call(
        leak_rows,
        f32(row_total // 2, LANES),
        5,
        scratch=(
            scratch(2, row_total // 2, LANES),
            scratch(2, row_total, LANES),
            scratch(row_total, LANES),
        ),
        micros=3,
    )(found, ends, cells, beds, info)
    arrived = lax.all_to_all(sent, AXES, split_axis=0, concat_axis=0, tiled=True)
    head_field, routed = call(
        everywhere,
        (f32(layers, rows, width), f32(row_total, reaches)),
        10,
        scratch=(
            scratch(2, 2, layers, pads, LANES),
            scratch(7, 2, layers, tall, LANES),
            scratch(2, layers, pads, LANES),
            scratch(reaches // LANES, row_total, LANES),
            sides,
        ),
        mib=20,
        micros=5,
    )(*fields, *pair_x, *pair_y, row_reach, route_inverse[0])
    reach_flow = call(finish_flow, f32(1, reaches), 2)(arrived, routed)
    return (head_field, reach_flow)


def solution(mesh):
    placed = (
        P(None, "gx", "gy"),
        P(None, "gx", "gy"),
        P(None, "gx", "gy"),
        P(None, "gx", "gy"),
        P("gx", "gy"),
        P(AXES, None, None),
        P(AXES, None),
        P(AXES, None),
        P(AXES, None),
        P(AXES, None, None),
        P(AXES),
        P(AXES),
    )
    return jax.shard_map(
        per_device,
        mesh=mesh,
        in_specs=placed,
        out_specs=(P(None, "gx", "gy"), P(AXES, None)),
        check_vma=False,
    )
```

```python
import functools

import jax
import jax.numpy as jnp
from jax import lax
from jax.experimental import pallas as pl
from jax.experimental.pallas import tpu as pltpu
from jax.sharding import PartitionSpec as P

SWEEPS = 8
HALO = 8
LANES = 128
GROUPS = LANES // HALO
AXES = ("gx", "gy")
VMEM = pl.BlockSpec(memory_space=pltpu.VMEM)
ANY = pl.BlockSpec(memory_space=pl.ANY)
TOP, BOTTOM = HALO, 2 * HALO


def call(body, out, count, scratch=(), anywhere=False, mib=8, micros=1):
    return pl.pallas_call(
        body,
        out_shape=out,
        in_specs=[ANY if anywhere else VMEM] * count,
        out_specs=jax.tree.map(lambda _: VMEM, out),
        scratch_shapes=list(scratch),
        compiler_params=pltpu.CompilerParams(vmem_limit_bytes=mib * 1024 * 1024),
        cost_estimate=pl.CostEstimate(
            flops=0, transcendentals=0, bytes_accessed=micros * 3_000_000
        ),
    )


def f32(*shape):
    return jax.ShapeDtypeStruct(shape, jnp.float32)


def front(
    head, cond, source, storage, reach, section, depth, route, retention, heads,
    last_out, first_out, info_out,
    reach_here, section_here, depth_here, weight_here, retention_here, heads_here, sems,
):
    rows = head.shape[1]
    reaches = section.shape[1]
    edges = []
    for k, ref in enumerate((head, cond, source, storage)):
        edges.append((ref.at[:, rows - HALO :, :], last_out.at[k]))
        edges.append((ref.at[:, :HALO, :], first_out.at[k]))
    small = [
        (reach, reach_here),
        (section, section_here),
        (depth, depth_here),
        (route.at[0, reaches - 8 :, :], weight_here),
        (retention, retention_here),
        (heads, heads_here),
    ]
    copies = [pltpu.make_async_copy(a, b, sems.at[i]) for i, (a, b) in enumerate(small + edges)]
    for copy in copies:
        copy.start()
    for copy in copies[: len(small)]:
        copy.wait()
    carry = retention_here[0] * (1.0 - heads_here[0].astype(jnp.float32))
    sec = section_here[...]
    table = jnp.concatenate(
        [sec, sec - depth_here[...], weight_here[7:8, :], jnp.full((5, reaches), carry)], 0
    )
    count = reach.shape[1]
    for part in range(count // LANES):
        spots = jnp.broadcast_to(reach_here[:, part * LANES : (part + 1) * LANES], (8, LANES))
        picked = jnp.zeros((8, LANES), jnp.float32)
        for block in range(reaches // LANES):
            value = jnp.take_along_axis(
                table[:, block * LANES : (block + 1) * LANES],
                spots & (LANES - 1),
                axis=1,
                mode="promise_in_bounds",
            )
            picked = jnp.where(spots // LANES == block, value, picked)
        tall = jnp.concatenate([picked, jnp.zeros((LANES - 8, LANES), jnp.float32)], 0)
        info_out[part * LANES : (part + 1) * LANES, :] = jnp.transpose(tall)
    for copy in copies[len(small) :]:
        copy.wait()


def pack_y(head, cond, source, storage, low, high, even_out, odd_out):
    fields = (head, cond, source, storage)
    layers, rows, width = head.shape
    even_y = lax.axis_index("gy") % 2 == 0
    lane = lax.broadcasted_iota(jnp.int32, (rows + 2 * HALO, LANES), 1)
    first_sum = [None] * even_out.shape[0]
    last_sum = [None] * even_out.shape[0]
    for k in range(4):
        for l in range(layers):
            plane, group = divmod(k * layers + l, GROUPS)
            whole = tall_row(fields, (low, high), k, l)
            spread = turned(whole, group * HALO)
            if first_sum[plane] is None:
                first_sum[plane], last_sum[plane] = spread, spread
            else:
                first_sum[plane] = jnp.where(
                    lane // HALO == group, spread, first_sum[plane]
                )
                last_sum[plane] = jnp.where(
                    lane // HALO == (group - 1) % GROUPS, spread, last_sum[plane]
                )
    for plane in range(even_out.shape[0]):
        even_out[plane] = jnp.where(even_y, last_sum[plane], first_sum[plane])
        odd_out[plane] = jnp.where(even_y, first_sum[plane], last_sum[plane])


def cell_block(cells_ref, b):
    c, g = divmod(b, cells_ref.shape[0] // 16)
    cells = cells_ref[pl.ds(g * 16 + c, 8, stride=2), :]
    return cells & (LANES - 1), cells // LANES


def select(found, column, line, table):
    for r, spread in enumerate(table):
        value = jnp.take_along_axis(spread, column, axis=1, mode="promise_in_bounds")
        found = jnp.where(line == r, value, found)
    return found


def spread_rows(table):
    return [jnp.broadcast_to(table[r : r + 1, :], (8, LANES)) for r in range(table.shape[0])]


def tall_row(fields, beside_x, k, l):
    low, high = beside_x
    return jnp.concatenate([low[k, l], fields[k][l], high[k, l]], 0)


def settle(one, other, sides):
    even = lax.axis_index("gy") % 2 == 0
    for plane in range(sides.shape[1]):
        sides[0, plane] = jnp.where(even, other[plane], one[plane])
        sides[1, plane] = jnp.where(even, one[plane], other[plane])


def turned(value, by):
    return pltpu.roll(value, by % LANES, 1) if by % LANES else value


def side_tiles(fields, beside_x, sides):
    layers = fields[0].shape[0]

    def get(k, l):
        plane, group = divmod(k * layers + l, GROUPS)
        whole = tall_row(fields, beside_x, k, l)
        lane = lax.broadcasted_iota(jnp.int32, whole.shape, 1)
        both = jnp.where(lane // HALO == group, sides[1, plane], sides[0, plane])
        near = (lane < HALO) | (lane >= LANES - HALO)
        side = jnp.where(near, turned(both, -group * HALO), 0.0)
        return [whole, side]

    return get


def strip_tiles(strips, sides, layers):
    def get(k, l):
        plane, group = divmod(k * layers + l, GROUPS)
        lane = lax.broadcasted_iota(jnp.int32, sides.shape[2:], 1)
        after = turned(sides[1, plane], 2 * HALO - group * HALO)
        ahead = turned(sides[0, plane], 3 * HALO - (group - 1) % GROUPS * HALO)
        own = strips[k, l]
        inner = jnp.where(lane < 3 * HALO, after, ahead)
        return [jnp.where((lane >= 2 * HALO) & (lane < 4 * HALO), inner, own)]

    return get


def inside_rows(row):
    at_x = lax.axis_index("gx")
    first_row = jnp.where(at_x == 0, HALO, 0)
    last_row = jnp.where(at_x == lax.axis_size("gx") - 1, row.shape[0] - HALO, row.shape[0])
    return (row >= first_row) & (row < last_row)


def beside(tiles):
    lane = lax.broadcasted_iota(jnp.int32, tiles[0].shape, 1)
    ahead = [pltpu.roll(one, LANES - 1, 1) for one in tiles]
    behind = [pltpu.roll(one, 1, 1) for one in tiles]
    if len(tiles) == 1:
        return ahead, behind
    east = [jnp.where(lane == LANES - 1, ahead[1 - t], ahead[t]) for t in range(2)]
    west = [jnp.where(lane == 0, behind[1 - t], behind[t]) for t in range(2)]
    return east, west


def set_coefs(get, conds, coef, l, bottom):
    tiles, rows = conds.shape[0], conds.shape[2]
    span = slice(TOP, rows - TOP)
    east, west = beside([conds[t, l, span, :] for t in range(tiles)])
    storage, source = get(3, l), get(2, l)
    for t in range(tiles):
        mid = conds[t, l, span, :]
        inside = mid > 0.0

        def face(near):
            return jnp.where(inside & (near > 0.0), 0.5 * (mid + near), 0.0)

        faces = [
            face(east[t]),
            face(west[t]),
            face(conds[t, l, TOP + 1 : rows - TOP + 1, :]),
            face(conds[t, l, TOP - 1 : rows - TOP - 1, :]),
            0.5 * (mid + conds[t, l - 1, span, :]) if l else None,
            None if bottom else 0.5 * (mid + conds[t, l + 1, span, :]),
        ]
        total = storage[t]
        for one in faces:
            if one is not None:
                total = total + one
        inverse = jnp.where(inside, 1.0 / jnp.where(inside, total, 1.0), 0.0)
        for k, one in enumerate(faces):
            if one is not None:
                coef[k, t, l] = one * inverse
        coef[6, t, l] = source[t] * inverse


def relax(get, masks, heads, coef, conds, layers, cone, final):
    tiles, held, rows = heads.shape[1:4]
    edge = jnp.zeros((TOP, LANES), jnp.float32)
    for l in range(held):
        for t, value in enumerate(get(0, l)):
            heads[0, t, l, TOP : rows - TOP, :] = value
        for t, value in enumerate(get(1, l)):
            conds[t, l, TOP : rows - TOP, :] = jnp.where(masks[t], value, 0.0)
            for span in (slice(0, TOP), slice(rows - TOP, rows)):
                conds[t, l, span, :] = edge
                heads[0, t, l, span, :] = edge
                heads[1, t, l, span, :] = edge
    for l in range(held - 1 if cone else held):
        set_coefs(get, conds, coef, l, l + 1 == layers)
    for time in range(SWEEPS):
        last_sweep = time == SWEEPS - 1
        margin = BOTTOM if last_sweep else TOP
        many = SWEEPS - time if cone else layers
        old = time % 2
        for start in range(margin, rows - margin, 8):
            span = slice(start, start + 8)
            mids = [
                [heads[old, t, l, span, :] for t in range(tiles)]
                for l in range(min(many + 1, layers))
            ]
            for l in range(many):
                east, west = beside(mids[l])
                at = slice(start - TOP, start - TOP + 8)
                for t in range(1 if last_sweep else tiles):
                    out = coef[6, t, l, at, :] + coef[0, t, l, at, :] * east[t]
                    out = out + coef[1, t, l, at, :] * west[t]
                    out = out + coef[2, t, l, at, :] * heads[old, t, l, start + 1 : start + 9, :]
                    out = out + coef[3, t, l, at, :] * heads[old, t, l, start - 1 : start + 7, :]
                    if l:
                        out = out + coef[4, t, l, at, :] * mids[l - 1][t]
                    if l + 1 < layers:
                        out = out + coef[5, t, l, at, :] * mids[l + 1][t]
                    if last_sweep:
                        final(l, start - BOTTOM, out)
                    else:
                        heads[1 - old, t, l, span, :] = out


def inner(
    head, cond, source, storage, low, high, cells, bed,
    beds_out, found_out, strips_out, heads, coef, conds, top,
):
    fields = (head, cond, source, storage)
    beside_x = (low, high)
    layers, rows, width = head.shape
    tall = rows + 2 * HALO
    lane = lax.broadcasted_iota(jnp.int32, (tall, LANES), 1)
    for k in range(4):
        for l in range(SWEEPS + 1 if k < 2 else SWEEPS):
            whole = tall_row(fields, beside_x, k, l)
            strip = jnp.where(lane < 2 * HALO, turned(whole, 2 * HALO), turned(whole, 4 * HALO))
            strips_out[k, l] = jnp.where(lane < 6 * HALO, strip, 0.0)

    def final(l, start, value):
        top[start : start + 8, :] = value

    inside = inside_rows(lax.broadcasted_iota(jnp.int32, (tall, LANES), 0))
    relax(
        lambda k, l: [tall_row(fields, beside_x, k, l)], [inside],
        heads, coef, conds, layers, True, final,
    )
    bed_table, head_table = spread_rows(bed[...]), spread_rows(top[...])
    for b in range(cells.shape[0] // 8):
        column, line = cell_block(cells, b)
        span = slice(b * 8, (b + 1) * 8)
        nothing = jnp.zeros((8, LANES), jnp.float32)
        beds_out[span, :] = select(nothing, column, line, bed_table)
        found_out[span, :] = select(nothing, column, line, head_table)


def edges(layers, strips, other_y, one_y, ends_out, heads, coef, conds, sides):
    settle(one_y, other_y, sides)
    tall = strips.shape[2]
    lane = lax.broadcasted_iota(jnp.int32, (tall, LANES), 1)
    at_y = lax.axis_index("gy")
    first = (at_y == 0) & (lane >= 3 * HALO) & (lane < 4 * HALO)
    last = (at_y == lax.axis_size("gy") - 1) & (lane >= 2 * HALO) & (lane < 3 * HALO)
    inside = inside_rows(lax.broadcasted_iota(jnp.int32, (tall, LANES), 0))
    mask = inside & ~first & ~last & (lane < 6 * HALO)

    def final(l, start, value):
        column = lax.broadcasted_iota(jnp.int32, value.shape, 1)
        row = lax.broadcasted_iota(jnp.int32, value.shape, 0)
        ends = jnp.where(column < HALO, turned(value, -4 * HALO), value)
        ends = jnp.where(column < 2 * HALO, ends, 0.0)
        line = jnp.zeros_like(value)
        for r in range(8):
            line = line + jnp.where(row == r, turned(ends, r * 2 * HALO), 0.0)
        ends_out[start // 8 : start // 8 + 1, :] = jnp.sum(line, 0, keepdims=True)

    relax(
        strip_tiles(strips, sides, layers), [mask],
        heads, coef, conds, layers, True, final,
    )


def leak_rows(found, ends, cells, beds, info, send_out, weights, levels, leaks):
    peers = info.shape[0] // 2
    groups = peers // 8
    for c in range(2):
        for g in range(groups):
            detail = info[pl.ds(g * 16 + c, 8, stride=2), :]
            span = slice((c * groups + g) * 8, (c * groups + g + 1) * 8)
            for k in range(2):
                levels[k, span, :] = jnp.broadcast_to(detail[:, k : k + 1], (8, LANES))

    def running(value, lane, length):
        step = 1
        while step < length:
            value = value * jnp.where(lane % length >= step, pltpu.roll(value, step, 1), 1.0)
            step *= 2
        return value

    sub = lax.broadcasted_iota(jnp.int32, (peers, LANES), 0)
    lane = lax.broadcasted_iota(jnp.int32, (peers, LANES), 1)
    details = [info[pl.ds(c, peers, stride=2), :] for c in range(2)]
    carry_row = jnp.sum(jnp.where(sub == lane, details[0][:, 3:4], 0.0), 0, keepdims=True)
    sub, lane = sub[:8], lane[:8]
    within = running(jnp.where(lane % 8 > sub, carry_row, 1.0), lane, 8)
    own = jnp.where(lane % 8 > sub, within, 0.0)
    block = lax.broadcasted_iota(jnp.int32, (groups, LANES), 0)
    wide = lax.broadcasted_iota(jnp.int32, (groups, LANES), 1)
    beyond = running(jnp.where(wide > block * 8 + 7, carry_row, 1.0), wide, LANES)
    for g in range(groups):
        through = within[:, g * 8 + 7 : g * 8 + 8] * beyond[g : g + 1, :]
        product = jnp.where(lane // 8 == g, own, jnp.where(lane // 8 > g, through, 0.0))
        for c in range(2):
            weights[c, g * 8 : (g + 1) * 8, :] = product * details[c][g * 8 : (g + 1) * 8, 2:3]

    table = spread_rows(ends[...])
    for b in range(2 * groups):
        column, line = cell_block(cells, b)
        span = slice(b * 8, (b + 1) * 8)
        near = (column < HALO) | (column >= LANES - HALO)
        at = line * (2 * HALO) + jnp.where(column < HALO, column, column - (LANES - 2 * HALO))
        value = select(
            found[span, :], at & (LANES - 1), jnp.where(near, at // LANES, -1), table
        )
        leaks[span, :] = beds[span, :] * (
            jnp.maximum(value, levels[1, span, :]) - levels[0, span, :]
        )
    eight = lax.broadcasted_iota(jnp.int32, (8, LANES), 1)
    flow = jnp.zeros((8, LANES), jnp.float32)
    sums = []
    for g in range(groups):
        span = slice(g * 8, (g + 1) * 8)
        row_leak = [
            jnp.sum(leaks[c * peers + g * 8 : c * peers + (g + 1) * 8, :], 1, keepdims=True)
            for c in range(2)
        ]
        for c in range(2):
            flow = flow + weights[c, span, :] * row_leak[c]
        sums.append(jnp.where(eight == 0, row_leak[0], row_leak[1]))
    flow = jnp.sum(flow, 0, keepdims=True)
    for g in range(groups):
        mine = lax.broadcasted_iota(jnp.int32, (8, LANES), 0) + g * 8 == eight
        column = jnp.sum(jnp.where(mine, flow, 0.0), 1, keepdims=True)
        send_out[g * 8 : (g + 1) * 8, :] = jnp.where(eight == 2, column, sums[g])


def edge_leaks(
    layers, strips, other_y, one_y, found, cells, beds, info,
    send_out, heads, coef, conds, sides, ends, weights, levels, leaks,
):
    edges(layers, strips, other_y, one_y, ends, heads, coef, conds, sides)
    leak_rows(found, ends, cells, beds, info, send_out, weights, levels, leaks)


def everywhere(
    head, cond, source, storage, low, high, other_y, one_y, reach, route,
    field_out, routed_out, heads, coef, conds, lines, sides,
):
    fields = (head, cond, source, storage)
    beside_x = (low, high)
    settle(one_y, other_y, sides)
    layers, rows, width = head.shape
    tall = rows + 2 * HALO
    lane = lax.broadcasted_iota(jnp.int32, (tall, LANES), 1)
    inside = inside_rows(lax.broadcasted_iota(jnp.int32, (tall, LANES), 0))
    at_y = lax.axis_index("gy")
    after = jnp.where(at_y == lax.axis_size("gy") - 1, 0, HALO)
    ahead = jnp.where(at_y == 0, LANES, LANES - HALO)

    def final(l, start, value):
        field_out[l, start : start + 8, :] = value

    relax(
        side_tiles(fields, beside_x, sides),
        [inside, inside & ((lane < after) | (lane >= ahead))],
        heads, coef, conds, layers, False, final,
    )
    count, reaches = routed_out.shape
    line = lax.broadcasted_iota(jnp.int32, (reaches, count), 0)
    routed = lax.dot_general(
        (line == reach[...]).astype(jnp.float32),
        route[...],
        (((0,), (1,)), ((), ())),
        precision=lax.Precision.HIGHEST,
        preferred_element_type=jnp.float32,
    )
    for part in range(reaches // LANES):
        lines[part] = routed[:, part * LANES : (part + 1) * LANES]
    for part in range(reaches // LANES):
        for c in range(2):
            routed_out[c * (count // 2) : (c + 1) * (count // 2), part * LANES : (part + 1) * LANES] = (
                lines[part, pl.ds(c, count // 2, stride=2), :]
            )


def finish_flow(arrived, routed, out):
    half = arrived.shape[0]
    parts = arrived[...]
    flow = parts[:, 0:1] * routed[:half, :] + parts[:, 1:2] * routed[half:, :]
    out[...] = jnp.sum(flow + parts[:, 2:3], 0, keepdims=True)


def shifted(value, axis, by):
    count = lax.axis_size(axis)
    return lax.ppermute(value, axis, [(i, (i + by) % count) for i in range(count)])


def swapped(value, axis, first):
    count = lax.axis_size(axis)
    to = list(range(count))
    for i in range(first, count, 2):
        to[i], to[(i + 1) % count] = (i + 1) % count, i
    return lax.ppermute(value, axis, list(enumerate(to)))


def per_device(
    initial_head, conductivity, source_rate, storage_term, bed_conduct, row_cells, row_reach,
    river_section, bed_depth, route_inverse, retention, chain_heads,
):
    layers, rows, width = initial_head.shape
    fields = (initial_head, conductivity, source_rate, storage_term)
    edge = f32(4, layers, HALO, width)
    planes = -(-4 * layers // GROUPS)
    tall = rows + 2 * HALO
    side = f32(planes, tall, LANES)
    row_total = row_cells.shape[1]
    reaches = river_section.shape[1]
    cells = row_cells[0]

    def scratch(*shape):
        return pltpu.VMEM(shape, jnp.float32)

    last, first, info = call(
        front,
        (edge, edge, f32(row_total, LANES)),
        10,
        scratch=(
            pltpu.VMEM((1, row_total), jnp.int32),
            scratch(1, reaches),
            scratch(1, reaches),
            scratch(8, reaches),
            pltpu.SMEM((1,), jnp.float32),
            pltpu.SMEM((1,), jnp.int32),
            pltpu.SemaphoreType.DMA((14,)),
        ),
        anywhere=True,
        mib=60,
    )(*fields, row_reach, river_section, bed_depth, route_inverse, retention, chain_heads)
    pair_x = (shifted(last, "gx", 1), shifted(first, "gx", -1))
    info = lax.all_to_all(info, AXES, split_axis=0, concat_axis=0, tiled=True)
    for_even, for_odd = call(pack_y, (side, side), 6)(*fields, *pair_x)
    pair_y = (swapped(for_odd, "gy", 1), swapped(for_even, "gy", 0))
    pads = tall + 2 * TOP
    held = SWEEPS + 1
    sides = scratch(2, planes, tall, LANES)
    own = (
        scratch(2, 1, held, pads, LANES),
        scratch(7, 1, SWEEPS, tall, LANES),
        scratch(1, held, pads, LANES),
    )
    beds, found, strips = call(
        inner,
        (f32(row_total, LANES), f32(row_total, LANES), f32(4, held, tall, LANES)),
        8,
        scratch=(*own, scratch(rows, LANES)),
        mib=16,
        micros=3,
    )(*fields, *pair_x, cells, bed_conduct)
    sent = call(
        functools.partial(edge_leaks, layers),
        f32(row_total // 2, LANES),
        7,
        scratch=(
            *own,
            sides,
            scratch(rows // 8, LANES),
            scratch(2, row_total // 2, LANES),
            scratch(2, row_total, LANES),
            scratch(row_total, LANES),
        ),
        mib=16,
        micros=5,
    )(strips, *pair_y, found, cells, beds, info)
    arrived = lax.all_to_all(sent, AXES, split_axis=0, concat_axis=0, tiled=True)
    head_field, routed = call(
        everywhere,
        (f32(layers, rows, width), f32(row_total, reaches)),
        10,
        scratch=(
            scratch(2, 2, layers, pads, LANES),
            scratch(7, 2, layers, tall, LANES),
            scratch(2, layers, pads, LANES),
            scratch(reaches // LANES, row_total, LANES),
            sides,
        ),
        mib=20,
        micros=5,
    )(*fields, *pair_x, *pair_y, row_reach, route_inverse[0])
    reach_flow = call(finish_flow, f32(1, reaches), 2)(arrived, routed)
    return (head_field, reach_flow)


def solution(mesh):
    placed = (
        P(None, "gx", "gy"),
        P(None, "gx", "gy"),
        P(None, "gx", "gy"),
        P(None, "gx", "gy"),
        P("gx", "gy"),
        P(AXES, None, None),
        P(AXES, None),
        P(AXES, None),
        P(AXES, None),
        P(AXES, None, None),
        P(AXES),
        P(AXES),
    )
    return jax.shard_map(
        per_device,
        mesh=mesh,
        in_specs=placed,
        out_specs=(P(None, "gx", "gy"), P(AXES, None)),
        check_vma=False,
    )
```
